32 devices in a mesh: dp: 4 (over z), fsdp: 8 (over y, x, core).
Axes of the slice: x: 2, y: 2, z: 4, core: 2. Of those that a mesh axis runs over, the one named last changes fastest.
Arguments:
- tokens: bfloat16 [32768, 512], P(('dp', 'fsdp')), may hold values from -6 to 6
- segments: int32 [32768], P(('dp', 'fsdp')), may hold values from -1 to 8, as said below
- cotangent: bfloat16 [32768, 512], P(('dp', 'fsdp')), may hold values from -6 to 6
- w_qkv: bfloat16 [512, 1536], P('fsdp'), may hold values from -0.25 to 0.25
- w_out: bfloat16 [512, 512], P('fsdp'), may hold values from -2 to 2
- w_up: bfloat16 [512, 2048], P('fsdp'), may hold values from -0.25 to 0.25
- w_down: bfloat16 [2048, 512], P('fsdp'), may hold values from -0.125 to 0.125
- q_bias: bfloat16 [512], P('fsdp'), may hold values from -3 to 3
- v_bias: bfloat16 [512], P('fsdp'), may hold values from -3 to 3
- out_bias: bfloat16 [512], P('fsdp'), may hold values from -3 to 3
- up_bias: bfloat16 [2048], P('fsdp'), may hold values from -3 to 3
- down_bias: bfloat16 [512], P('fsdp'), may hold values from -3 to 3
- norm1_gain: bfloat16 [512], P('fsdp'), may hold values from 0.099609375 to 1.8984375
- norm1_bias: bfloat16 [512], P('fsdp'), may hold values from -3 to 3
- norm2_gain: bfloat16 [512], P('fsdp'), may hold values from 0.099609375 to 1.8984375
- norm2_bias: bfloat16 [512], P('fsdp'), may hold values from -3 to 3
Outputs:
- mixed: bfloat16 [32768, 512], P(('dp', 'fsdp'))
- tokens_grad: bfloat16 [32768, 512], P(('dp', 'fsdp'))
- qkv_grad: float32 [512, 1536], P('fsdp')
- out_grad: float32 [512, 512], P('fsdp')
- up_grad: float32 [512, 2048], P('fsdp')
- down_grad: float32 [2048, 512], P('fsdp')
- q_bias_grad: float32 [512], P('fsdp')
- v_bias_grad: float32 [512], P('fsdp')
- out_bias_grad: float32 [512], P('fsdp')
- up_bias_grad: float32 [2048], P('fsdp')
- down_bias_grad: float32 [512], P('fsdp')
- norm1_gain_grad: float32 [512], P('fsdp')
- norm1_bias_grad: float32 [512], P('fsdp')
- norm2_gain_grad: float32 [512], P('fsdp')
- norm2_bias_grad: float32 [512], P('fsdp')
The draws below stay inside these ranges and needn't reach their ends.
Inputs may be any that keep to these rules, and one draw needn't show every extreme that they name: `segments`: within each device's 1024 slots the images lie from the first slot on in order of their number, and the empty slots (-1) follow them. Image 0 of a device has 512 or 64 tokens, every other image 64, at most one image of a device has 512, and every device holds one image or more. Some device's slots are all full and some device has empty slots.
All inputs are finite; a program needn't handle non-finite values.
Results may differ from the reference program's by a relative error of at most 0.018.
Values may be sent and summed in bfloat16 or wider, within the bound.
No kernel may reach another device: no remote copies, remote signals or barrier semaphores. Data moves between devices by JAX's collectives and lax.ppermute only.
A program may use at most 128 MiB of HBM per device.

```python
import jax
import jax.numpy as jnp
from jax import lax

D = 512
HEADS = 8
HEAD_DIM = 64
FF = 2048
IMG_LEN = 512
THUMB = 64
TOK_DEV = 1024
TOKENS = 32768


def draw_segments(key, part):
    device_count = TOKENS // TOK_DEV
    most_thumbs = IMG_LEN // THUMB
    key_big, key_thumb, key_pick = jax.random.split(key, 3)
    has_big = jax.random.randint(key_big, (device_count,), 0, 2)
    thumbs = jax.random.randint(key_thumb, (device_count,), max(1, most_thumbs // 4), most_thumbs + 1)
    chosen = jax.random.permutation(key_pick, device_count)
    device_ids = jnp.arange(device_count)
    has_big = jnp.where(device_ids == chosen[0], 1, jnp.where(device_ids == chosen[1], 0, has_big))
    thumbs = jnp.where(device_ids == chosen[0], most_thumbs, thumbs)
    slot_ids = jnp.arange(TOK_DEV)[None, :]
    offset = slot_ids - (has_big * IMG_LEN)[:, None]
    image_id = offset // THUMB + has_big[:, None]
    filled = offset < (thumbs * THUMB)[:, None]
    result = jnp.where(offset < 0, 0, jnp.where(filled, image_id, -1))
    return result.reshape(-1).astype(jnp.int32)


def block_levels(rng, dims, shards, smallest, high):
    gain = 1.0
    for axis_at, shards_of in shards:
        draws = jax.random.uniform(jax.random.fold_in(jax.random.fold_in(rng, 6), axis_at), (shards_of,), jnp.float32, smallest / len(shards), high / len(shards))
        gain = gain * jnp.repeat(jnp.exp(draws), dims[axis_at] // shards_of).reshape((-1,) + (1,) * (len(dims) - 1 - axis_at))
    return gain


def gaussian(own_key, shape, scale, reach, cuts=(), kind=jnp.bfloat16):
    array = scale * jax.random.normal(own_key, shape, jnp.float32)
    if cuts:
        array = array * block_levels(own_key, shape, cuts, -0.22, 0.18)
    return jnp.clip(array, -reach, reach).astype(kind)


def setup_inputs(seed: int = 0) -> dict:
    seeds = jax.random.split(jax.random.key(seed), 17)
    tokens = gaussian(seeds[0], (TOKENS, D), 1.0, 6.0, ((0, 32),))
    segments = draw_segments(jax.random.fold_in(seeds[16], 71), 0)
    cotangent = gaussian(seeds[2], (TOKENS, D), 1.0, 6.0, ((0, 32),))
    w_qkv = gaussian(seeds[3], (D, 3 * D), D ** -0.5, 0.25, ((0, 8),))
    w_out = gaussian(seeds[4], (D, D), (D // 64) ** -0.5, 2.0, ((0, 8),))
    w_up = gaussian(seeds[5], (D, FF), D ** -0.5, 0.25, ((0, 8),))
    w_down = gaussian(seeds[6], (FF, D), FF ** -0.5, 0.125, ((0, 8),))
    q_bias = gaussian(seeds[7], (D,), 0.5, 3.0, ((0, 8),))
    v_bias = gaussian(seeds[8], (D,), 0.5, 3.0, ((0, 8),))
    out_bias = gaussian(seeds[9], (D,), 0.5, 3.0, ((0, 8),))
    up_bias = gaussian(seeds[10], (FF,), 0.5, 3.0, ((0, 8),))
    down_bias = gaussian(seeds[11], (D,), 0.5, 3.0, ((0, 8),))
    norm1_gain = jnp.clip(1.0 + 0.18 * jax.random.normal(seeds[12], (D,), jnp.float32), 0.099609375, 1.8984375).astype(jnp.bfloat16)
    norm1_bias = gaussian(seeds[13], (D,), 0.5, 3.0, ((0, 8),))
    norm2_gain = jnp.clip(1.0 + 0.18 * jax.random.normal(seeds[14], (D,), jnp.float32), 0.099609375, 1.8984375).astype(jnp.bfloat16)
    norm2_bias = gaussian(seeds[15], (D,), 0.5, 3.0, ((0, 8),))
    return {"tokens": tokens, "segments": segments, "cotangent": cotangent, "w_qkv": w_qkv, "w_out": w_out, "w_up": w_up, "w_down": w_down, "q_bias": q_bias, "v_bias": v_bias, "out_bias": out_bias, "up_bias": up_bias, "down_bias": down_bias, "norm1_gain": norm1_gain, "norm1_bias": norm1_bias, "norm2_gain": norm2_gain, "norm2_bias": norm2_bias}


MASKED_SCORE = -1e+30
NORM_EPSILON = 1e-05

@jax.custom_vjp
def low(v):
    return lax.optimization_barrier(v.astype(jnp.bfloat16)).astype(jnp.float32)

@jax.custom_vjp
def low_back(v):
    return v

def low_keep(v):
    return (low(v), None)

def low_pass(kept, grad):
    return (grad,)

def back_keep(v):
    return (v, None)

def back_low(kept, grad):
    return (low(grad),)
low.defvjp(low_keep, low_pass)
low_back.defvjp(back_keep, back_low)

def layer_norm(values, norm_gain, norm_shift):
    centre = lax.optimization_barrier(jnp.mean(values, -1, keepdims=True))
    centred = values - centre
    spread = lax.optimization_barrier(jnp.mean(centred * centred, -1, keepdims=True))
    return centred * lax.rsqrt(spread + NORM_EPSILON) * norm_gain + norm_shift

def attend(queries, seg_rows, keys_all, values_all, seg_all):
    scores = jnp.einsum('qhd,khd->hqk', queries, keys_all, precision=lax.Precision.HIGHEST) * 0.125
    scores = low_back(scores)
    same_image = seg_rows[:, None] == seg_all[None, :]
    scores = jnp.where(same_image[None], scores, MASKED_SCORE)
    row_max = lax.optimization_barrier(jnp.max(scores, -1, keepdims=True))
    raised = jnp.exp(scores - row_max)
    chances = raised / lax.optimization_barrier(jnp.sum(raised, -1, keepdims=True))
    return jnp.einsum('hqk,khd->qhd', low(chances), values_all, precision=lax.Precision.HIGHEST)

def forward(segments_dev, inputs, w_qkv, w_out, w_up, w_down, q_bias, v_bias, out_bias, up_bias, down_bias, norm1_gain, norm1_bias, norm2_gain, norm2_bias):
    row_count = inputs.shape[0]
    block_rows = min(512, row_count)
    blocks = row_count // block_rows
    normed = low(layer_norm(inputs, norm1_gain, norm1_bias))
    projected = jnp.dot(normed, w_qkv, precision=lax.Precision.HIGHEST)
    queries = low_back(low(projected[:, :D] + q_bias))
    keys_all = low_back(low(projected[:, D:2 * D]))
    values_all = low_back(low(projected[:, 2 * D:] + v_bias))
    shaped_queries = queries.reshape(blocks, block_rows, HEADS, HEAD_DIM)
    shaped_keys = keys_all.reshape(row_count, HEADS, HEAD_DIM)
    shaped_values = values_all.reshape(row_count, HEADS, HEAD_DIM)
    seg_blocks = segments_dev.reshape(blocks, block_rows)
    checked = jax.checkpoint(attend)
    attended = lax.map(lambda pieces: checked(pieces[0], pieces[1], shaped_keys, shaped_values, segments_dev), (shaped_queries, seg_blocks))
    attended = low_back(low(attended.reshape(row_count, D)))
    branch = low_back(jnp.dot(attended, w_out, precision=lax.Precision.HIGHEST) + out_bias)
    middle = inputs + branch
    normed_two = low(layer_norm(middle, norm2_gain, norm2_bias))
    hidden = low_back(jnp.dot(normed_two, w_up, precision=lax.Precision.HIGHEST) + up_bias)
    activated = low(jax.nn.gelu(hidden, approximate=True))
    mlp_out = low_back(jnp.dot(activated, w_down, precision=lax.Precision.HIGHEST) + down_bias)
    return middle + mlp_out

def reference(tokens, segments, cotangent, w_qkv, w_out, w_up, w_down, q_bias, v_bias, out_bias, up_bias, down_bias, norm1_gain, norm1_bias, norm2_gain, norm2_bias):
    params = tuple((item.astype(jnp.float32) for item in (w_qkv, w_out, w_up, w_down, q_bias, v_bias, out_bias, up_bias, down_bias, norm1_gain, norm1_bias, norm2_gain, norm2_bias)))
    groups = TOKENS // TOK_DEV
    input_blocks = tokens.astype(jnp.float32).reshape(groups, TOK_DEV, D)
    seg_blocks = segments.reshape(groups, TOK_DEV)
    cot_blocks = cotangent.astype(jnp.float32).reshape(groups, TOK_DEV, D)

    def one_device(totals, pieces):
        inputs, seg_dev, cot_dev = pieces
        live_rows = (seg_dev >= 0)[:, None]
        result, back_fn = jax.vjp(lambda *operands: forward(seg_dev, *operands), inputs, *params)
        grads = back_fn(jnp.where(live_rows, cot_dev, 0.0))
        mixed_dev = jnp.where(live_rows, result, 0.0).astype(jnp.bfloat16)
        totals = tuple((left + right for left, right in zip(totals, grads[1:])))
        return (totals, (mixed_dev, grads[0].astype(jnp.bfloat16)))
    empty_grads = tuple((jnp.zeros(item.shape, jnp.float32) for item in params))
    totals, (mixed, grad_inputs) = lax.scan(one_device, empty_grads, (input_blocks, seg_blocks, cot_blocks))
    return (mixed.reshape(TOKENS, D), grad_inputs.reshape(TOKENS, D), totals[0], totals[1], totals[2], totals[3], totals[4], totals[5], totals[6], totals[7], totals[8], totals[9], totals[10], totals[11], totals[12])
```

```python
import functools
import math

import jax
import jax.numpy as jnp
from jax import lax
from jax.experimental import pallas as pl
from jax.experimental.pallas import tpu as pltpu
from jax.sharding import PartitionSpec as P

D = 512
HEADS = 8
HD = 64
FF = 2048
HALF = 512
DB = 128
BIAS = 16
EPS = 1e-05
MASKED = -1e30
F32 = jnp.float32
BF = jnp.bfloat16
LOG2E = math.log2(math.e)
QSCALE = 0.125 * LOG2E
LN2 = math.log(2.0)
NN = (((1,), (0,)), ((), ()))
NT = (((1,), (1,)), ((), ()))
TN = (((0,), (0,)), ((), ()))
VM = pl.BlockSpec(memory_space=pltpu.VMEM)
SM = pl.BlockSpec(memory_space=pltpu.SMEM)
QB, VB, OB, DBI, G1, C1, G2, C2, UB = range(9)


def mm(a, b, dims):
    return lax.dot_general(a, b, dims, preferred_element_type=F32)


def run(body, ins, outs, scratch=(), smem=(), flops=0, vmem=56):
    specs = [SM if i in smem else VM for i in range(len(ins))]
    size = sum(math.prod(a.shape) * a.dtype.itemsize for a in ins) + sum(
        math.prod(s) * jnp.dtype(d).itemsize for s, d in outs
    )
    return pl.pallas_call(
        body,
        out_shape=[jax.ShapeDtypeStruct(s, d) for s, d in outs],
        in_specs=specs,
        out_specs=[VM] * len(outs),
        scratch_shapes=list(scratch),
        compiler_params=pltpu.CompilerParams(vmem_limit_bytes=vmem * 2**20),
        cost_estimate=pl.CostEstimate(flops=flops, bytes_accessed=size, transcendentals=0),
    )(*ins)


def step_bits(n):
    bits = [1 << p for p in range(1, n.bit_length() - 1)]
    return bits[::-1], bits


def masks(bits):
    k = len(bits)
    found = []
    for s in range(1 << k):
        m = 0
        for p in range(k):
            if not (s >> (k - 1 - p)) & 1:
                m ^= bits[p]
        found.append(m)
    return found


def swap_core(x, n):
    return lax.ppermute(x, "fsdp", [(i, i ^ 1) for i in range(n)])


def swap_step(x, n, p):
    even, odd = step_bits(n)
    return lax.ppermute(x, "fsdp", [(i, i ^ (odd[p] if i & 1 else even[p])) for i in range(n)])


def gather(x, n):
    have = [x]
    for p in reversed(range(len(step_bits(n)[0]))):
        have = have + [swap_step(t, n, p) for t in have]
    own = have[::-1]
    return own + [swap_core(t, n) for t in own]


def add_parts(parts, rows):
    def body(*refs):
        out = refs[-1]
        total = None
        for ref, (_, first) in zip(refs[:-1], parts):
            v = ref[first : first + rows, :].astype(F32)
            total = v if total is None else total + v
        out[...] = total.astype(BF)

    return run(body, [a for a, _ in parts], [((rows, D), BF)])[0]


def scatter_sum(send, keeps, n):
    got = [(swap_core(send, n), 0)]
    for p, keep in enumerate(keeps):
        rows = keep.shape[0]
        mine = add_parts([(keep, 0)] + got, rows)
        if p == len(keeps) - 1:
            return mine
        got = [(a, f + rows) for a, f in got]
        got.append((swap_step(mine, n, p), 0))


def dp_sum(x, d):
    if d & (d - 1):
        return lax.psum(x, "dp")
    k = 1
    while k < d:
        x = add_parts([(x, 0), (lax.ppermute(x, "dp", [(i, i ^ k) for i in range(d)]), 0)], x.shape[0])
        k *= 2
    return x


def norm_stats(x):
    mu = jnp.mean(x, -1, keepdims=True)
    c = x - mu
    rs = lax.rsqrt(jnp.mean(c * c, -1, keepdims=True) + EPS)
    return c * rs, rs


def softmax_rows(s):
    m = jnp.max(s, 0, keepdims=True)
    e = jnp.exp2(s - m)
    return e.astype(BF), 1.0 / jnp.sum(e, 0, keepdims=True)


def same_block(seg_ref, b):
    row = jnp.broadcast_to(seg_ref[:, b * DB : (b + 1) * DB].astype(F32), (DB, DB))
    return row == row.T


def attn_fwd_kernel(n, rows, meta, x, seg, *refs):
    pieces = refs[:n]
    bias_o, w_o, h1_o, q_o, k_o, v_o, kt_o, ot_o, linv_o, e_o, ed_o, vt = refs[n:]
    t = x.shape[0]
    wide = 3 * rows
    lane = lax.broadcasted_iota(jnp.int32, (BIAS, D), 1) // (D // n)
    bias = jnp.zeros((BIAS, D), F32)
    ub = [jnp.zeros((1, D), F32) for _ in range(4)]
    for r in range(n):
        j = meta[r]
        for c in range(3):
            w_o[pl.ds(pl.multiple_of(j * rows, rows), rows), c * D : (c + 1) * D] = pieces[r][
                c * rows : (c + 1) * rows, :
            ]
        got = pieces[r][wide : wide + BIAS, :].astype(F32)
        bias = jnp.where(lane == j, got, bias)
        for c in range(4):
            at = c * (n // 4) + lax.broadcasted_iota(jnp.int32, (1, D), 1) // (FF // n)
            ub[c] = jnp.where(at == j, got[UB : UB + 1, :], ub[c])
    bias_o[0:BIAS, :] = bias
    for c in range(4):
        bias_o[UB + c : UB + c + 1, :] = ub[c]

    tile = 256
    for i in range(t // tile):
        at = slice(i * tile, (i + 1) * tile)
        nrm, _ = norm_stats(x[at, :].astype(F32))
        h1 = (nrm * bias[G1 : G1 + 1, :] + bias[C1 : C1 + 1, :]).astype(BF)
        h1_o[at, :] = h1
        q_o[at, :] = ((mm(h1, w_o[:, :D], NN) + bias[QB : QB + 1, :]) * QSCALE).astype(BF)
        k = mm(h1, w_o[:, D : 2 * D], NN).astype(BF)
        k_o[at, :] = k
        kt_o[:, at] = k.T
        v = (mm(h1, w_o[:, 2 * D :], NN) + bias[VB : VB + 1, :]).astype(BF)
        v_o[at, :] = v
        vt[:, at] = v.T

    big = meta[n] == 1

    @pl.when(big)
    def _():
        for h in range(HEADS):
            hs = slice(h * HD, (h + 1) * HD)
            e, linv = softmax_rows(mm(k_o[:HALF, hs], q_o[:HALF, hs], NT))
            e_o[h] = e
            ot_o[hs, :HALF] = (mm(vt[hs, :HALF], e, NN) * linv).astype(BF)
            linv_o[h : h + 1, :HALF] = linv

    def diagonal(blocks):
        for b in blocks:
            at = slice(b * DB, (b + 1) * DB)
            same = same_block(seg, b)
            for h in range(HEADS):
                hs = slice(h * HD, (h + 1) * HD)
                s = mm(k_o[at, hs], q_o[at, hs], NT)
                e, linv = softmax_rows(jnp.where(same, s, MASKED))
                ed_o[h, b] = e
                ot_o[hs, at] = (mm(vt[hs, at], e, NN) * linv).astype(BF)
                linv_o[h : h + 1, at] = linv

    @pl.when(jnp.logical_not(big))
    def _():
        diagonal(range(HALF // DB))

    diagonal(range(HALF // DB, t // DB))


def place_rows(meta, n, pieces, first, rows, out, col=0, width=D):
    for r in range(n):
        j = meta[r]
        out[pl.ds(pl.multiple_of(j * rows, rows), rows), col : col + width] = pieces[r][first : first + rows, :]


def slot_rows(meta, n, s):
    return meta[s]


def mlp_up_kernel(n, rows, meta, x, ot, bias, gm, *refs):
    pieces = refs[:n]
    wo_o, wu_o, x2_o, h2_o, z_o, gd_o, send_o = refs[n : n + 7]
    keeps = refs[n + 7 : -1]
    acc = refs[-1]
    t = x.shape[0]
    place_rows(meta, n, pieces, 0, rows, wo_o)
    for c in range(4):
        place_rows(meta, n, pieces, (1 + c) * rows, rows, wu_o, c * D)
    tile = 256
    ck = math.sqrt(2.0 / math.pi)
    for i in range(t // tile):
        at = slice(i * tile, (i + 1) * tile)
        x2 = x[at, :].astype(F32) + mm(ot[:, at], wo_o[...], TN) + bias[OB : OB + 1, :]
        x2_o[at, :] = x2
        nrm, _ = norm_stats(x2)
        h2 = (nrm * bias[G2 : G2 + 1, :] + bias[C2 : C2 + 1, :]).astype(BF)
        h2_o[at, :] = h2
        for c in range(4):
            cs = slice(c * D, (c + 1) * D)
            u = mm(h2, wu_o[:, cs], NN) + bias[UB + c : UB + c + 1, :]
            u2 = u * u
            h = 0.5 * jnp.tanh(u * (ck + (ck * 0.044715) * u2)) + 0.5
            z = u * h
            gd = h + z * (1.0 - h) * (2.0 * ck + (6.0 * ck * 0.044715) * u2)
            z_o[at, cs] = z.astype(BF)
            gd_o[at, cs] = gd.astype(BF)
    acc[...] = mm(z_o[...], gm[...], TN).astype(BF)
    fr = FF // n
    emit(meta, n, send_o, keeps, fr, lambda j, dst, lo: put_rows(acc, j, fr, dst, lo))


def put_rows(src, j, rows, dst, lo):
    dst[lo : lo + rows, :] = src[pl.ds(pl.multiple_of(j * rows, rows), rows), :]


def emit(meta, n, send_o, keeps, rows, put):
    s = 0
    for ref in keeps:
        for i in range(ref.shape[0] // rows):
            put(meta[s], ref, i * rows)
            s += 1
    for i in range(n // 2):
        put(meta[n // 2 + i], send_o, i * rows)


def mlp_back_kernel(n, rows, meta, x2, ot, bias, gm, h2, gd, wo, wu, linv, *refs):
    pieces = refs[:n]
    wd_o, ga_o, got_o, drow_o, bg_o, send_o = refs[n : n + 6]
    keeps = refs[n + 6 : -3]
    gu, acc_up, acc_out = refs[-3:]
    t = x2.shape[0]
    fr = FF // n
    place_rows(meta, n, pieces, 0, fr, wd_o)
    tile = 256
    g2s = jnp.zeros((1, D), F32)
    c2s = jnp.zeros((1, D), F32)
    obs = jnp.zeros((1, D), F32)
    dbs = jnp.zeros((1, D), F32)
    ubs = [jnp.zeros((1, D), F32) for _ in range(4)]
    for i in range(t // tile):
        at = slice(i * tile, (i + 1) * tile)
        g = gm[at, :]
        dbs += jnp.sum(g.astype(F32), 0, keepdims=True)
        for c in range(4):
            cs = slice(c * D, (c + 1) * D)
            part = (mm(g, wd_o[cs, :], NT) * gd[at, cs].astype(F32)).astype(BF)
            gu[at, cs] = part
            ubs[c] += jnp.sum(part.astype(F32), 0, keepdims=True)
        r2 = mm(gu[at, :], wu[...], NT)
        nrm, rs = norm_stats(x2[at, :])
        g2s += jnp.sum(r2 * nrm, 0, keepdims=True)
        c2s += jnp.sum(r2, 0, keepdims=True)
        dn = r2 * bias[G2 : G2 + 1, :]
        dv = rs * (dn - jnp.mean(dn, -1, keepdims=True) - nrm * jnp.mean(dn * nrm, -1, keepdims=True))
        ga = (g.astype(F32) + dv).astype(BF)
        ga_o[at, :] = ga
        obs += jnp.sum(ga.astype(F32), 0, keepdims=True)
        go = mm(wo[...], ga, NT)
        for h in range(HEADS):
            hs = slice(h * HD, (h + 1) * HD)
            gs = (go[hs, :] * linv[h : h + 1, at]).astype(BF)
            got_o[hs, at] = gs
            drow_o[h : h + 1, at] = jnp.sum(gs.astype(F32) * ot[hs, at].astype(F32), 0, keepdims=True)
    bg_o[...] = jnp.zeros_like(bg_o)
    bg_o[OB : OB + 1, :] = obs
    bg_o[DBI : DBI + 1, :] = dbs
    bg_o[G2 : G2 + 1, :] = g2s
    bg_o[C2 : C2 + 1, :] = c2s
    for c in range(4):
        bg_o[UB + c : UB + c + 1, :] = ubs[c]
    acc_out[...] = mm(ot[...], ga_o[...], NN).astype(BF)
    acc_up[...] = mm(h2[...], gu[...], TN).astype(BF)

    def put(j, dst, lo):
        put_rows(acc_out, j, rows, dst, lo)
        here = pl.ds(pl.multiple_of(j * rows, rows), rows)
        for c in range(4):
            dst[lo + (1 + c) * rows : lo + (2 + c) * rows, :] = acc_up[here, c * D : (c + 1) * D]

    emit(meta, n, send_o, keeps, 5 * rows, put)


def attn_back_kernel(n, rows, meta, x, bias, h1, q, k, v, kt, e, ed, got, drow, wq, bg, *refs):
    dv_o, send_o = refs[:2]
    keeps = refs[2:-3]
    g, gqt, acc = refs[-3:]
    t = x.shape[0]
    big = meta[n] == 1

    def one(at, hs, h, prob):
        dp = mm(v[at, hs], got[hs, at], NN)
        ds = (prob.astype(F32) * (dp - drow[h : h + 1, at])).astype(BF)
        gqt[hs, at] = (mm(kt[hs, at], ds, NN) * 0.125).astype(BF)
        g[at, D + h * HD : D + (h + 1) * HD] = (mm(ds, q[at, hs], NN) * LN2).astype(BF)
        g[at, 2 * D + h * HD : 2 * D + (h + 1) * HD] = mm(prob, got[hs, at], NT).astype(BF)

    @pl.when(big)
    def _():
        for h in range(HEADS):
            one(slice(0, HALF), slice(h * HD, (h + 1) * HD), h, e[h])

    def diagonal(blocks):
        for b in blocks:
            for h in range(HEADS):
                one(slice(b * DB, (b + 1) * DB), slice(h * HD, (h + 1) * HD), h, ed[h, b])

    @pl.when(jnp.logical_not(big))
    def _():
        diagonal(range(HALF // DB))

    diagonal(range(HALF // DB, t // DB))
    g[:, :D] = gqt[...].T

    tile = 256
    g1s = jnp.zeros((1, D), F32)
    c1s = jnp.zeros((1, D), F32)
    qbs = jnp.zeros((1, D), F32)
    vbs = jnp.zeros((1, D), F32)
    for i in range(t // tile):
        at = slice(i * tile, (i + 1) * tile)
        qbs += jnp.sum(g[at, :D].astype(F32), 0, keepdims=True)
        vbs += jnp.sum(g[at, 2 * D :].astype(F32), 0, keepdims=True)
        r1 = mm(g[at, :], wq[...], NT)
        nrm, rs = norm_stats(x[at, :].astype(F32))
        g1s += jnp.sum(r1 * nrm, 0, keepdims=True)
        c1s += jnp.sum(r1, 0, keepdims=True)
        dn = r1 * bias[G1 : G1 + 1, :]
        dv_o[at, :] = rs * (dn - jnp.mean(dn, -1, keepdims=True) - nrm * jnp.mean(dn * nrm, -1, keepdims=True))
    acc[...] = mm(h1[...], g[...], TN).astype(BF)
    row = lax.broadcasted_iota(jnp.int32, (BIAS, D), 0)
    full = bg[...]
    for at, val in ((QB, qbs), (VB, vbs), (G1, g1s), (C1, c1s)):
        full = jnp.where(row == at, val, full)
    full = full.astype(BF)

    def put(j, dst, lo):
        here = pl.ds(pl.multiple_of(j * rows, rows), rows)
        for c in range(3):
            dst[lo + c * rows : lo + (1 + c) * rows, :] = acc[here, c * D : (c + 1) * D]
        dst[lo + 3 * rows : lo + 3 * rows + BIAS, :] = full

    emit(meta, n, send_o, keeps, 3 * rows + BIAS, put)


def finish_kernel(x2, z, wd, bias, livec, ga, dv, mixed_o, tg_o):
    t = x2.shape[0]
    tile = 256
    for i in range(t // tile):
        at = slice(i * tile, (i + 1) * tile)
        out = x2[at, :] + mm(z[at, :], wd[...], NN) + bias[DBI : DBI + 1, :]
        mixed_o[at, :] = jnp.where(livec[at, :] >= 0, out, 0.0).astype(BF)
        tg_o[at, :] = (ga[at, :].astype(F32) + dv[at, :]).astype(BF)


def on_device(n, d, tokens, segments, cotangent, w_qkv, w_out, w_up, w_down, *vectors):
    t = tokens.shape[0]
    rows = w_qkv.shape[0]
    fr = w_down.shape[0]
    me = lax.axis_index("fsdp")
    odd = (me & 1) == 1
    even_bits, odd_bits = step_bits(n)
    own = jnp.where(odd, jnp.array(masks(odd_bits), jnp.int32), jnp.array(masks(even_bits), jnp.int32))
    sib = jnp.where(odd, jnp.array(masks(even_bits), jnp.int32), jnp.array(masks(odd_bits), jnp.int32))
    big = (segments[HALF - 1] == 0).astype(jnp.int32)
    meta = jnp.concatenate([own ^ me, sib ^ (me ^ 1), big[None]]).astype(jnp.int32)

    qb, vb, ob, ub, db, g1, c1, g2, c2 = vectors
    lines = [jnp.tile(a, D // a.shape[0]) for a in (qb, vb, ob, db, g1, c1, g2, c2, ub)]
    lines = jnp.pad(jnp.stack(lines), ((0, BIAS - len(lines)), (0, 0)))
    pack_a = jnp.concatenate([w_qkv[:, c * D : (c + 1) * D] for c in range(3)] + [lines], 0)
    pack_b = jnp.concatenate([w_out] + [w_up[:, c * D : (c + 1) * D] for c in range(4)], 0)

    got_a = gather(pack_a, n)
    got_b = gather(pack_b, n)
    got_c = gather(w_down, n)

    live = (segments >= 0)[:, None]
    gm = jnp.where(live, cotangent, jnp.zeros_like(cotangent))
    seg_row = segments[None, :]

    nb = t // DB
    bias, wq, h1, q, k, v, kt, ot, linv, e, ed = run(
        functools.partial(attn_fwd_kernel, n, rows),
        [meta, tokens, seg_row] + got_a,
        [
            ((BIAS, D), F32),
            ((D, 3 * D), BF),
            ((t, D), BF),
            ((t, D), BF),
            ((t, D), BF),
            ((t, D), BF),
            ((D, t), BF),
            ((D, t), BF),
            ((HEADS, t), F32),
            ((HEADS, HALF, HALF), BF),
            ((HEADS, nb, DB, DB), BF),
        ],
        [pltpu.VMEM((D, t), BF)],
        smem=(0,),
        flops=6 * 10**9,
    )

    steps = len(even_bits)
    counts = [1 << (steps - 1 - p) for p in range(steps)] + [1]

    def slots(r):
        return [((n // 2 * r, D), BF)] + [((c * r, D), BF) for c in counts]

    wo, wu, x2, h2, z, gd, *down = run(
        functools.partial(mlp_up_kernel, n, rows),
        [meta, tokens, ot, bias, gm] + got_b,
        [((D, D), BF), ((D, FF), BF), ((t, D), F32), ((t, D), BF), ((t, FF), BF), ((t, FF), BF)] + slots(fr),
        [pltpu.VMEM((FF, D), BF)],
        smem=(0,),
        flops=5 * 10**9,
    )
    down = scatter_sum(down[0], down[1:], n)

    r_b = 5 * rows
    wd, ga, got, drow, bg, *up = run(
        functools.partial(mlp_back_kernel, n, rows),
        [meta, x2, ot, bias, gm, h2, gd, wo, wu, linv] + got_c,
        [((FF, D), BF), ((t, D), BF), ((D, t), BF), ((HEADS, t), F32), ((BIAS, D), F32)] + slots(r_b),
        [pltpu.VMEM((t, FF), BF), pltpu.VMEM((D, FF), BF), pltpu.VMEM((D, D), BF)],
        smem=(0,),
        flops=8 * 10**9,
    )
    up = scatter_sum(up[0], up[1:], n)

    dv, *last = run(
        functools.partial(attn_back_kernel, n, rows),
        [meta, tokens, bias, h1, q, k, v, kt, e, ed, got, drow, wq, bg],
        [((t, D), F32)] + slots(3 * rows + BIAS),
        [pltpu.VMEM((t, 3 * D), BF), pltpu.VMEM((D, t), BF), pltpu.VMEM((D, 3 * D), BF)],
        smem=(0,),
        flops=8 * 10**9,
    )
    last = scatter_sum(last[0], last[1:], n)

    mixed, tokens_grad = run(
        finish_kernel,
        [x2, z, wd, bias, segments[:, None], ga, dv],
        [((t, D), BF), ((t, D), BF)],
        flops=2 * 10**9,
    )

    down, up, last = dp_sum(down, d), dp_sum(up, d), dp_sum(last, d)
    part = D // n
    first = me * part
    vec = lax.dynamic_slice(last, (3 * rows, first), (BIAS, part)).astype(F32)
    ubg = lax.dynamic_slice(last[3 * rows + UB : 3 * rows + UB + 4, :].reshape(-1), (me * fr,), (fr,)).astype(F32)
    qkv_grad = jnp.concatenate([last[c * rows : (c + 1) * rows] for c in range(3)], 1).astype(F32)
    up_grad = jnp.concatenate([up[(1 + c) * rows : (2 + c) * rows] for c in range(4)], 1).astype(F32)
    return (
        mixed,
        tokens_grad,
        qkv_grad,
        up[:rows].astype(F32),
        up_grad,
        down.astype(F32),
        vec[QB],
        vec[VB],
        vec[OB],
        ubg,
        vec[DBI],
        vec[G1],
        vec[C1],
        vec[G2],
        vec[C2],
    )


def solution(mesh):
    rows = P(("dp", "fsdp"), None)
    mat, vec = P("fsdp", None), P("fsdp")
    return jax.shard_map(
        functools.partial(on_device, mesh.shape["fsdp"], mesh.shape["dp"]),
        mesh=mesh,
        in_specs=(rows, P(("dp", "fsdp")), rows) + (mat,) * 4 + (vec,) * 9,
        out_specs=(rows, rows) + (mat,) * 4 + (vec,) * 9,
        check_vma=False,
    )
```

```python
import functools
import math

import jax
import jax.numpy as jnp
from jax import lax
from jax.experimental import pallas as pl
from jax.experimental.pallas import tpu as pltpu
from jax.sharding import PartitionSpec as P

D = 512
HEADS = 8
HD = 64
FF = 2048
HALF = 512
DB = 128
BIAS = 16
EPS = 1e-05
MASKED = -1e30
F32 = jnp.float32
BF = jnp.bfloat16
LOG2E = math.log2(math.e)
QSCALE = 0.125 * LOG2E
LN2 = math.log(2.0)
CK = math.sqrt(2.0 / math.pi)
CA = 0.044715
NN = (((1,), (0,)), ((), ()))
NT = (((1,), (1,)), ((), ()))
TN = (((0,), (0,)), ((), ()))

SM = pl.BlockSpec(memory_space=pltpu.SMEM)
QB, VB, OB, DBI, G1, C1, G2, C2, UB = range(9)


def mm(a, b, dims):
    return lax.dot_general(a, b, dims, preferred_element_type=F32)


class Copies:
    def __init__(self, sems):
        self.sems, self.used, self.out = sems, 0, []

    def start(self, src, dst):
        copy = pltpu.make_async_copy(src, dst, self.sems.at[self.used])
        self.used += 1
        copy.start()
        return copy

    def send(self, src, dst):
        self.out.append(self.start(src, dst))

    def finish(self):
        for copy in self.out:
            copy.wait()


class Held:
    def __init__(self, copies, src, buf):
        self.buf, self.copies = buf, [copies.start(src, buf)]

    @property
    def ref(self):
        for copy in self.copies:
            copy.wait()
        self.copies = []
        return self.buf


SPECS = {"S": SM, "A": pl.BlockSpec(memory_space=pltpu.HBM), "V": pl.BlockSpec(memory_space=pltpu.VMEM)}


def run(body, ins, outs, bufs=(), sems=64, flops=0, name=None, room=6):
    n_in, n_out = len(ins), len(outs)

    def kernel(*refs):
        copies = Copies(refs[-1])
        body(copies, refs[:n_in], refs[n_in : n_in + n_out], refs[n_in + n_out : -1])
        copies.finish()

    size = sum(math.prod(a.shape) * a.dtype.itemsize for a, _ in ins) + sum(
        math.prod(o[0]) * jnp.dtype(o[1]).itemsize for o in outs
    )
    scratch = sum(math.prod(shape) * jnp.dtype(d).itemsize for shape, d in bufs)
    return pl.pallas_call(
        kernel,
        out_shape=[jax.ShapeDtypeStruct(o[0], o[1]) for o in outs],
        in_specs=[SPECS[k] for _, k in ins],
        out_specs=[SPECS[o[2]] for o in outs],
        scratch_shapes=[pltpu.VMEM(shape, d) for shape, d in bufs] + [pltpu.SemaphoreType.DMA((sems,))],
        compiler_params=pltpu.CompilerParams(vmem_limit_bytes=scratch + room * 2**20),
        cost_estimate=pl.CostEstimate(flops=flops, bytes_accessed=size, transcendentals=0),
        name=name,
    )(*ins_only(ins))


def ins_only(ins):
    return [a for a, _ in ins]


def kind(k, *arrays):
    return [(a, k) for a in arrays]


def step_bits(n):
    bits = [1 << p for p in range(1, n.bit_length() - 1)]
    return bits[::-1], bits


def masks(bits):
    k = len(bits)
    found = []
    for s in range(1 << k):
        m = 0
        for p in range(k):
            if not (s >> (k - 1 - p)) & 1:
                m ^= bits[p]
        found.append(m)
    return found


def swap_core(x, n):
    return lax.ppermute(x, "fsdp", [(i, i ^ 1) for i in range(n)])


def swap_step(x, n, p):
    even, odd = step_bits(n)
    return lax.ppermute(x, "fsdp", [(i, i ^ (odd[p] if i & 1 else even[p])) for i in range(n)])


def after(x, *others):
    return lax.optimization_barrier((x,) + others)[0]


def gather_masks(n):
    return list(range(0, n, 2)) + list(range(1, n, 2))


class Gather:
    def __init__(self, x, n):
        self.n = n
        self.have = [x] + [lax.ppermute(x, "fsdp", [(i, i ^ m) for i in range(n)]) for m in range(2, n, 2)]

    def pieces(self, *others):
        return self.have + [swap_core(after(t, *others), self.n) for t in self.have]


def add_parts(parts, rows):
    total = sum(a[f : f + rows].astype(F32) for a, f in parts)
    return lax.optimization_barrier(total.astype(BF))


def swap_dp(x, n, d, even, odd):
    pairs = []
    for z in range(d):
        for i in range(n):
            pairs.append((z * n + i, (z ^ (odd if i & 1 else even)) * n + i))
    return lax.ppermute(x, ("dp", "fsdp"), pairs)


def dp_steps(d):
    bits = [1 << p for p in range(d.bit_length() - 1)]
    return list(zip(bits, bits[::-1]))


class Sum:
    def __init__(self, n, d, send, keeps):
        self.n, self.d, self.keeps, self.step = n, d, keeps, 0
        self.got = [(swap_core(send, n), 0)]
        self.own = None
        self.dp = dp_steps(d) if d & (d - 1) == 0 else None

    def advance(self, *others):
        if self.step < len(self.keeps):
            keep = self.keeps[self.step]
            rows = keep.shape[0]
            mine = add_parts([(after(keep, *others), 0)] + self.got, rows)
            self.got = [(a, f + rows) for a, f in self.got]
            if self.step < len(self.keeps) - 1:
                self.got.append((swap_step(mine, self.n, self.step), 0))
            else:
                self.own = mine
                self.send_dp()
        else:
            rows = self.own.shape[0]
            mine = self.own = add_parts([(after(self.own, *others), 0), (self.arrive, 0)], rows)
            self.send_dp()
        self.step += 1
        return mine

    def send_dp(self):
        at = self.step - len(self.keeps) + 1
        if self.dp is None:
            self.own = lax.psum(self.own, "dp")
        elif at < len(self.dp):
            self.arrive = swap_dp(self.own, self.n, self.d, *self.dp[at])

    def end(self):
        last = len(self.keeps) + (0 if self.dp is None else len(self.dp))
        while self.step < last:
            self.advance()
        return self.own


def norm_stats(x):
    mu = jnp.mean(x, -1, keepdims=True)
    c = x - mu
    rs = lax.rsqrt(jnp.mean(c * c, -1, keepdims=True) + EPS)
    return c * rs, rs


def softmax_rows(s):
    m = jnp.max(s, 0, keepdims=True)
    e = jnp.exp2(s - m)
    return e.astype(BF), 1.0 / jnp.sum(e, 0, keepdims=True)


def same_block(seg_ref, b):
    row = jnp.broadcast_to(seg_ref[:, b * DB : (b + 1) * DB].astype(F32), (DB, DB))
    return row == row.T


def piece_block(n, r):
    return lax.axis_index("fsdp") ^ gather_masks(n)[r]


def slot_block(n, s):
    me = lax.axis_index("fsdp")
    even, odd = (masks(b) for b in step_bits(n))
    if s < n // 2:
        return me ^ jnp.where((me & 1) == 1, odd[s], even[s])
    s -= n // 2
    return me ^ 1 ^ jnp.where((me & 1) == 1, even[s], odd[s])


def is_big(seg_ref):
    last = seg_ref[:, HALF - 128 : HALF].astype(F32)
    lane = lax.broadcasted_iota(jnp.int32, (1, 128), 1)
    return jnp.max(jnp.where(lane == 127, last, -1.0)) == 0.0


def place(copies, n, pieces, first, rows, buf, col=0):
    started = []
    for r in range(n):
        here = pl.ds(pl.multiple_of(piece_block(n, r) * rows, rows), rows)
        started.append(copies.start(pieces[r].at[pl.ds(first, rows), :], buf.at[here, pl.ds(col, D)]))
    return started


def wait_all(started):
    for copy in started:
        copy.wait()


def pack_body(n, copies, ins, outs, bufs):
    wq, wo, wu = ins[:3]
    vecs = ins[3:]
    a_o, b_o = outs
    rows = wq.shape[0]
    a, b = bufs[:2]
    vbufs = bufs[2:]
    mats = [copies.start(wq.at[:, pl.ds(c * D, D)], a.at[pl.ds(c * rows, rows), :]) for c in range(3)]
    held = [Held(copies, v, vb) for v, vb in zip(vecs, vbufs)]
    rest = [copies.start(wo, b.at[pl.ds(0, rows), :])]
    for c in range(4):
        rest.append(copies.start(wu.at[:, pl.ds(c * D, D)], b.at[pl.ds((1 + c) * rows, rows), :]))
    full = []
    for h in held:
        g = h.ref[...].astype(F32).reshape(1, -1)
        full.append(jnp.concatenate([g] * (D // g.shape[1]), 1))
    full.append(jnp.zeros((BIAS - len(full), D), F32))
    a[pl.ds(3 * rows, BIAS), :] = jnp.concatenate(full, 0).astype(BF)
    wait_all(mats)
    copies.send(a, a_o)
    wait_all(rest)
    copies.send(b, b_o)


def qkv_body(n, rows, copies, ins, outs, bufs):
    x_h = ins[0]
    pieces = ins[1:]
    bias_b, w, h1_b, q, k, v, kt, vt = outs
    x, lines = bufs
    t = x.shape[0]
    x = Held(copies, x_h, x)
    vecs = [copies.start(pieces[r].at[pl.ds(3 * rows, BIAS), :], lines.at[r]) for r in range(n)]
    parts = [place(copies, n, pieces, c * rows, rows, w, c * D) for c in range(3)]
    wait_all(vecs)
    lane = lax.broadcasted_iota(jnp.int32, (BIAS, D), 1)
    bias = jnp.zeros((BIAS, D), F32)
    ub = [jnp.zeros((1, D), F32) for _ in range(4)]
    for r in range(n):
        j = piece_block(n, r)
        got = lines[r].astype(F32)
        bias = jnp.where(lane // (D // n) == j, got, bias)
        for c in range(4):
            ub[c] = jnp.where(c * (n // 4) + lane[:1, :] // (FF // n) == j, got[UB : UB + 1, :], ub[c])
    bias_b[0:BIAS, :] = bias
    for c in range(4):
        bias_b[UB + c : UB + c + 1, :] = ub[c]
    xr = x.ref
    tile = 256
    for i in range(t // tile):
        at = slice(i * tile, (i + 1) * tile)
        nrm, _ = norm_stats(xr[at, :].astype(F32))
        h1_b[at, :] = (nrm * bias[G1 : G1 + 1, :] + bias[C1 : C1 + 1, :]).astype(BF)
    for c, (buf, tbuf) in enumerate(((q, None), (k, kt), (v, vt))):
        wait_all(parts[c])
        for i in range(t // tile):
            at = slice(i * tile, (i + 1) * tile)
            got = mm(h1_b[at, :], w[:, c * D : (c + 1) * D], NN)
            if c == 0:
                got = (got + bias[QB : QB + 1, :]) * QSCALE
            if c == 2:
                got = got + bias[VB : VB + 1, :]
            got = got.astype(BF)
            buf[at, :] = got
            if tbuf is not None:
                tbuf[:, at] = got.T


def attn_body(n, copies, ins, outs, bufs):
    seg, q, k, vt = ins
    ot, linv_b, e_b, ed_b = outs
    t = q.shape[0]
    nh = HALF // DB
    big = is_big(seg)

    def head(h):
        return slice(h * HD, (h + 1) * HD)

    def finish(h, at, e, linv):
        ot[head(h), at] = (mm(vt[head(h), at], e, NN) * linv).astype(BF)
        linv_b[h : h + 1, at] = linv

    def dense():
        at = slice(0, HALF)
        ahead = mm(k[at, head(0)], q[at, head(0)], NT)
        for h in range(HEADS):
            s = ahead
            if h + 1 < HEADS:
                ahead = mm(k[at, head(h + 1)], q[at, head(h + 1)], NT)
            e, linv = softmax_rows(s)
            e_b[h] = e
            finish(h, at, e, linv)

    def diagonal(blocks):
        keys = [(b, h) for b in blocks for h in range(HEADS)]
        at = {b: slice(b * DB, (b + 1) * DB) for b in blocks}
        same = {b: same_block(seg, b) for b in blocks}
        s = [mm(k[at[b], head(h)], q[at[b], head(h)], NT) for b, h in keys]
        r = [softmax_rows(jnp.where(same[b], x, MASKED)) for (b, h), x in zip(keys, s)]
        for (b, h), (e, _) in zip(keys, r):
            if b < nh:
                e_b[h, at[b], :DB] = e
            else:
                ed_b[h, b - nh] = e
        for (b, h), (e, linv) in zip(keys, r):
            finish(h, at[b], e, linv)

    pl.when(big)(dense)

    @pl.when(jnp.logical_not(big))
    def _():
        for b in range(0, nh, 2):
            diagonal((b, b + 1))

    for b in range(nh, t // DB, 2):
        diagonal((b, b + 1))


def send_slots(copies, n, outs, rows, put):
    send_h, keeps = outs[0], outs[1:]
    s = 0
    for ref in list(keeps) + [send_h]:
        for i in range(ref.shape[0] // rows):
            put(slot_block(n, s), s, ref, i * rows)
            s += 1


def mlp_up_body(n, rows, copies, ins, outs, bufs):
    x_h, ot, bias, gm_h = ins[:4]
    pieces = ins[4:]
    wo, wu, x2, h2, z_h, gd = outs[:6]
    x, gm, z, acc = bufs
    t = x.shape[0]
    fr = FF // n
    started = place(copies, n, pieces, 0, rows, wo)
    x = Held(copies, x_h, x)
    ups = [place(copies, n, pieces, (1 + c) * rows, rows, wu, c * D) for c in range(4)]
    gm = Held(copies, gm_h, gm)
    wait_all(started)
    x = x.ref
    tile = 256
    for i in range(t // tile):
        at = slice(i * tile, (i + 1) * tile)
        x2[at, :] = x[at, :].astype(F32) + mm(ot[:, at], wo[...], TN) + bias[OB : OB + 1, :]
    gain, shift = bias[G2 : G2 + 1, :], bias[C2 : C2 + 1, :]
    for i in range(t // tile):
        at = slice(i * tile, (i + 1) * tile)
        nrm, _ = norm_stats(x2[at, :])
        h2[at, :] = (nrm * gain + shift).astype(BF)
    for c in range(4):
        wait_all(ups[c])
    for i in range(t // tile):
        at = slice(i * tile, (i + 1) * tile)
        for c in range(4):
            cs = slice(c * D, (c + 1) * D)
            v = mm(h2[at, :], wu[:, cs], NN) + bias[UB + c : UB + c + 1, :]
            v2 = v * v
            hh = 0.5 * jnp.tanh(v * (CK + (CK * CA) * v2)) + 0.5
            zz = v * hh
            z[at, cs] = zz.astype(BF)
            gd[at, cs] = (hh + zz * (1.0 - hh) * (2.0 * CK + (6.0 * CK * CA) * v2)).astype(BF)
    copies.send(z, z_h)
    gm = gm.ref

    per = D // fr
    for c in range(4):
        acc[pl.ds(c * per, per)] = mm(z[:, c * D : (c + 1) * D], gm[...], TN).astype(BF).reshape(per, fr, D)

    def put(j, s, dst, lo):
        copies.send(acc.at[j], dst.at[pl.ds(lo, fr), :])

    send_slots(copies, n, outs[6:], fr, put)


def mlp_back_body(n, rows, copies, ins, outs, bufs):
    gm_h, gd, wu, x2, bias, wo, linv, ot = ins[:8]
    pieces = ins[8:]
    wd_h, ga, got, drow, bg, gu = outs
    gm, wd, r2, go = bufs
    t = gm.shape[0]
    fr = FF // n
    gm = Held(copies, gm_h, gm)
    if len(pieces) == 1:
        wds = [copies.start(pieces[0], wd)]
    else:
        wds = place(copies, n, pieces, 0, fr, wd)
    gm = gm.ref
    wait_all(wds)
    copies.send(wd, wd_h)
    tile = 256
    ubs = [jnp.zeros((1, D), F32) for _ in range(4)]
    dbs = jnp.zeros((1, D), F32)
    for i in range(t // tile):
        at = slice(i * tile, (i + 1) * tile)
        g = gm[at, :]
        dbs += jnp.sum(g.astype(F32), 0, keepdims=True)
        for c in range(4):
            cs = slice(c * D, (c + 1) * D)
            part = (mm(g, wd[cs, :], NT) * gd[at, cs].astype(F32)).astype(BF)
            gu[at, cs] = part
            ubs[c] += jnp.sum(part.astype(F32), 0, keepdims=True)
    gain = bias[G2 : G2 + 1, :]
    for i in range(t // tile):
        at = slice(i * tile, (i + 1) * tile)
        r2[at, :] = mm(gu[at, :], wu[...], NT)

    g2s = c2s = obs = jnp.zeros((1, D), F32)
    for i in range(t // tile):
        at = slice(i * tile, (i + 1) * tile)
        r = r2[at, :]
        nrm, rs = norm_stats(x2[at, :])
        rn = r * nrm
        g2s += jnp.sum(rn, 0, keepdims=True)
        c2s += jnp.sum(r, 0, keepdims=True)
        dn = r * gain
        dv = rs * (dn - jnp.mean(dn, -1, keepdims=True) - nrm * jnp.mean(rn * gain, -1, keepdims=True))
        out = (gm[at, :].astype(F32) + dv).astype(BF)
        ga[at, :] = out
        obs += jnp.sum(out.astype(F32), 0, keepdims=True)
    for i in range(t // tile):
        at = slice(i * tile, (i + 1) * tile)
        go[...] = mm(wo[...], ga[at, :], NT)
        for h in range(HEADS):
            hs = slice(h * HD, (h + 1) * HD)
            gs = (go[hs, :] * linv[h : h + 1, at]).astype(BF)
            got[hs, at] = gs
            drow[h : h + 1, at] = jnp.sum(gs.astype(F32) * ot[hs, at].astype(F32), 0, keepdims=True)
    bg[...] = jnp.zeros_like(bg)
    bg[OB : OB + 1, :] = obs
    bg[DBI : DBI + 1, :] = dbs
    bg[G2 : G2 + 1, :] = g2s
    bg[C2 : C2 + 1, :] = c2s
    for c in range(4):
        bg[UB + c : UB + c + 1, :] = ubs[c]


def mlp_grad_body(n, rows, copies, ins, outs, bufs):
    ot, ga, h2, gu = ins
    acc_up, acc_out = bufs
    acc_out[...] = mm(ot[...], ga[...], NN).astype(BF)

    def put_out(j, s, dst, lo):
        here = pl.ds(pl.multiple_of(j * rows, rows), rows)
        copies.send(acc_out.at[here, :], dst.at[pl.ds(lo, rows), :])

    send_slots(copies, n, outs, 5 * rows, put_out)
    for c in range(4):
        cs = slice(c * D, (c + 1) * D)
        acc_up[:, cs] = mm(h2[...], gu[:, cs], TN).astype(BF)

        def put(j, s, dst, lo, c=c):
            here = pl.ds(pl.multiple_of(j * rows, rows), rows)
            copies.send(acc_up.at[here, pl.ds(c * D, D)], dst.at[pl.ds(lo + (1 + c) * rows, rows), :])

        send_slots(copies, n, outs, 5 * rows, put)


def head(h):
    return slice(h * HD, (h + 1) * HD)


def back_dense(e, v, got, drow, kt, q, gqt, gk, gv):
    at = slice(0, HALF)
    ahead = mm(v[at, head(0)], got[head(0), at], NN)
    for h in range(HEADS):
        hs, dp = head(h), ahead
        if h + 1 < HEADS:
            ahead = mm(v[at, head(h + 1)], got[head(h + 1), at], NN)
        prob = e[h]
        ds = (prob.astype(F32) * (dp - drow[h : h + 1, at])).astype(BF)
        gqt[hs, at] = (mm(kt[hs, at], ds, NN) * 0.125).astype(BF)
        gk[at, hs] = (mm(ds, q[at, hs], NN) * LN2).astype(BF)
        gv[at, hs] = mm(prob, got[hs, at], NT).astype(BF)


def back_blocks(blocks, prob, v, got, drow, kt, q, gqt, gk, gv):
    keys = [(b, h) for b in blocks for h in range(HEADS)]
    at = {b: slice(b * DB, (b + 1) * DB) for b in blocks}
    dp = [mm(v[at[b], head(h)], got[head(h), at[b]], NN) for b, h in keys]
    pv = [mm(prob(b, h), got[head(h), at[b]], NT) for b, h in keys]
    ds = [
        (prob(b, h).astype(F32) * (x - drow[h : h + 1, at[b]])).astype(BF) for (b, h), x in zip(keys, dp)
    ]
    pq = [mm(kt[head(h), at[b]], x, NN) for (b, h), x in zip(keys, ds)]
    pk = [mm(x, q[at[b], head(h)], NN) for (b, h), x in zip(keys, ds)]
    for i, (b, h) in enumerate(keys):
        gqt[head(h), at[b]] = (pq[i] * 0.125).astype(BF)
        gk[at[b], head(h)] = (pk[i] * LN2).astype(BF)
        gv[at[b], head(h)] = pv[i].astype(BF)


def attn_back_body(n, copies, ins, outs, bufs):
    seg, v, got, drow, e, kt, q = ins
    gqt, gk, gv = outs
    big = is_big(seg)

    @pl.when(big)
    def _():
        back_dense(e, v, got, drow, kt, q, gqt, gk, gv)

    @pl.when(jnp.logical_not(big))
    def _():
        def prob(b, h):
            return e[h, b * DB : (b + 1) * DB, :DB]

        for b in range(0, HALF // DB, 2):
            back_blocks((b, b + 1), prob, v, got, drow, kt, q, gqt, gk, gv)


def qkv_back_body(n, rows, copies, ins, outs, bufs):
    v, got, drow, ed, kt, q, gqt0, gk0, gv0, wq, x_h, bias, h1, bg = ins
    dv = outs[0]
    x, gqt, gk, gv, g, r1, acc, full_b = bufs
    x = Held(copies, x_h, x)
    t = x_h.shape[0]
    nb, nh = t // DB, HALF // DB
    for b in range(nh, nb, 2):
        back_blocks((b, b + 1), lambda b, h: ed[h, b - nh], v, got, drow, kt, q, gqt, gk, gv)
    g[:HALF, :D] = gqt0[...].T
    g[HALF:, :D] = gqt[:, HALF:].T
    g[:HALF, D : 2 * D] = gk0[...]
    g[HALF:, D : 2 * D] = gk[HALF:, :]
    g[:HALF, 2 * D :] = gv0[...]
    g[HALF:, 2 * D :] = gv[HALF:, :]

    tile = 256
    x = x.ref
    gain = bias[G1 : G1 + 1, :]
    for c in range(3):
        cs = slice(c * D, (c + 1) * D)
        acc[:, cs] = mm(h1[...], g[:, cs], TN).astype(BF)

        def put_mat(j, s, dst, lo, c=c):
            here = pl.ds(pl.multiple_of(j * rows, rows), rows)
            copies.send(acc.at[here, pl.ds(c * D, D)], dst.at[pl.ds(lo + c * rows, rows), :])

        send_slots(copies, n, outs[1:], 3 * rows + BIAS, put_mat)
    for i in range(t // tile):
        at = slice(i * tile, (i + 1) * tile)
        r1[at, :] = mm(g[at, :], wq[...], NT)
    g1s = c1s = qbs = vbs = jnp.zeros((1, D), F32)
    for i in range(t // tile):
        at = slice(i * tile, (i + 1) * tile)
        r = r1[at, :]
        nrm, rs = norm_stats(x[at, :].astype(F32))
        rn = r * nrm
        g1s += jnp.sum(rn, 0, keepdims=True)
        c1s += jnp.sum(r, 0, keepdims=True)
        qbs += jnp.sum(g[at, :D].astype(F32), 0, keepdims=True)
        vbs += jnp.sum(g[at, 2 * D :].astype(F32), 0, keepdims=True)
        dn = r * gain
        dv[at, :] = (
            rs * (dn - jnp.mean(dn, -1, keepdims=True) - nrm * jnp.mean(rn * gain, -1, keepdims=True))
        ).astype(BF)
    row = lax.broadcasted_iota(jnp.int32, (BIAS, D), 0)
    full = bg[...]
    for at, val in ((QB, qbs), (VB, vbs), (G1, g1s), (C1, c1s)):
        full = jnp.where(row == at, val, full)
    full_b[...] = full.astype(BF)

    def put(j, s, dst, lo):
        copies.send(full_b, dst.at[pl.ds(lo + 3 * rows, BIAS), :])

    send_slots(copies, n, outs[1:], 3 * rows + BIAS, put)


def finish_body(copies, ins, outs, bufs):
    z_h, wd_h, x2, bias, live, ga, dv = ins
    mixed_h, tg_h = outs
    z, wd, mixed, tg = bufs
    z, wd = Held(copies, z_h, z), Held(copies, wd_h, wd)
    t = mixed.shape[0]
    cols = jnp.broadcast_to(live[...].astype(F32), (128, t)).T
    tg[...] = (ga[...].astype(F32) + dv[...].astype(F32)).astype(BF)
    copies.send(tg, tg_h)
    z, wd = z.ref, wd.ref
    tile = 256
    for i in range(t // tile):
        at = slice(i * tile, (i + 1) * tile)
        out = x2[at, :] + mm(z[at, :], wd[...], NN) + bias[DBI : DBI + 1, :]
        mixed[at, :] = jnp.where(cols[at, :1] >= 0, out, 0.0).astype(BF)
    copies.send(mixed, mixed_h)


def on_device(n, d, tokens, segments, cotangent, w_qkv, w_out, w_up, w_down, *vectors):
    t = tokens.shape[0]
    rows = w_qkv.shape[0]
    fr = w_down.shape[0]
    nb, nh = t // DB, HALF // DB
    me = lax.axis_index("fsdp")
    qb, vb, ob, ub, db, g1, c1, g2, c2 = vectors
    lines = [qb, vb, ob, db, g1, c1, g2, c2, ub]
    ra, rb, rc = 3 * rows + BIAS, 5 * rows, fr
    pack_a, pack_b = run(
        functools.partial(pack_body, n),
        kind("A", w_qkv, w_out, w_up, *lines),
        [((ra, D), BF, "A"), ((rb, D), BF, "A")],
        [((ra, D), BF), ((rb, D), BF)] + [(a.shape, BF) for a in lines],
        name="pack",
        room=58,
    )
    a = Gather(pack_a, n)
    b = Gather(pack_b, n)
    got_a = a.pieces()
    c = Gather(after(w_down, a.have[1]), n)
    live = (segments >= 0)[:, None]
    gm = jnp.where(live, cotangent, jnp.zeros_like(cotangent))
    seg_row = segments[None, :]

    tok, tokt, wide = ((t, D), BF), ((D, t), BF), ((t, FF), BF)
    hrow, bias_s, tokf = ((HEADS, t), F32), ((BIAS, D), F32), ((t, D), F32)
    bias, wq, h1, q, k, v, kt, vt = run(
        functools.partial(qkv_body, n, rows),
        kind("A", tokens, *got_a),
        [o + ("V",) for o in (bias_s, ((D, 3 * D), BF), tok, tok, tok, tok, tokt, tokt)],
        [tok, ((n, BIAS, D), BF)],
        sems=96,
        flops=3 * 10**9,
        name="qkv",
    )
    ot, linv, e, ed = run(
        functools.partial(attn_body, n),
        kind("V", seg_row, q, k, vt),
        [o + ("V",) for o in (tokt, hrow, ((HEADS, HALF, HALF), BF), ((HEADS, nb - nh, DB, DB), BF))],
        flops=5 * 10**9,
        name="attn",
    )
    got_b = b.pieces(ot)

    steps = len(step_bits(n)[0])
    counts = [1 << (steps - 1 - p) for p in range(steps)] + [1]

    def slots(r):
        return [((n // 2 * r, D), BF, "A")] + [((m * r, D), BF, "A") for m in counts]

    wo, wu, x2, h2, z, gd, *down = run(
        functools.partial(mlp_up_body, n, rows),
        kind("A", tokens) + kind("V", ot, bias) + kind("A", gm, *got_b),
        [o + ("V",) for o in (((D, D), BF), ((D, FF), BF), tokf, tok)] + [wide + ("A",), wide + ("V",)] + slots(rc),
        [tok, tok, wide, ((n, rc, D), BF)],
        sems=128,
        flops=6 * 10**9,
        name="mlp_up",
    )
    got_c = c.pieces(h2)
    down = Sum(n, d, down[0], down[1:])

    wd, ga, got, drow, bg, gu = run(
        functools.partial(mlp_back_body, n, rows),
        kind("A", gm) + kind("V", gd, wu, x2, bias, wo, linv, ot) + kind("A", *got_c),
        [((FF, D), BF, "A")] + [o + ("V",) for o in (tok, tokt, hrow, bias_s, wide)],
        [tok, ((FF, D), BF), tokf, ((D, 256), F32)],
        flops=6 * 10**9,
        name="mlp_back",
    )
    s = down.advance(ga)
    up = run(
        functools.partial(mlp_grad_body, n, rows),
        kind("V", after(ot, s), ga, h2, gu),
        slots(rb),
        [((D, FF), BF), ((D, D), BF)],
        sems=128,
        flops=3 * 10**9,
        name="mlp_grad",
    )
    up_sent = up[0]
    up = Sum(n, d, up[0], up[1:])
    s = down.advance(up_sent)
    half, halft = ((HALF, D), BF), ((D, HALF), BF)
    gqt, gk, gv = run(
        functools.partial(attn_back_body, n),
        kind("V", seg_row, after(v, s), got, drow, e, kt, q),
        [o + ("V",) for o in (halft, half, half)],
        flops=4 * 10**9,
        name="attn_back",
    )
    s = down.advance(gk)
    r = up.advance(gk, s)
    dv, *last = run(
        functools.partial(qkv_back_body, n, rows),
        kind("V", after(v, s, r), got, drow, ed, kt, q, gqt, gk, gv, wq)
        + kind("A", tokens)
        + kind("V", bias, h1, bg),
        [tok + ("V",)] + slots(ra),
        [tok, tokt, tok, tok, ((t, 3 * D), BF), tokf, ((D, 3 * D), BF), ((BIAS, D), BF)],
        sems=128,
        flops=6 * 10**9,
        name="qkv_back",
    )
    last_sent = last[0]
    last = Sum(n, d, last[0], last[1:])

    mixed, tokens_grad = run(
        finish_body,
        kind("A", after(z, last_sent), wd) + kind("V", x2, bias, seg_row, ga, dv),
        [tok + ("A",), tok + ("A",)],
        [wide, ((FF, D), BF), tok, tok],
        flops=2 * 10**9,
        name="finish",
    )
    r = last.advance(mixed)
    s = up.advance(r)
    s = down.advance(s)
    r = last.advance(s)
    s = up.advance(r)
    r = last.advance(s)
    s = down.advance(r)
    s = up.advance(s)
    r = last.advance(s)
    down, up, last = down.end(), up.end(), last.end()
    part = D // n
    first = me * part
    vec = lax.dynamic_slice(last, (3 * rows, first), (BIAS, part)).astype(F32)
    ubg = lax.dynamic_slice(last[3 * rows + UB : 3 * rows + UB + 4, :].reshape(-1), (me * fr,), (fr,)).astype(F32)
    qkv_grad = jnp.concatenate([last[c * rows : (c + 1) * rows] for c in range(3)], 1).astype(F32)
    up_grad = jnp.concatenate([up[(1 + c) * rows : (2 + c) * rows] for c in range(4)], 1).astype(F32)
    return (
        mixed,
        tokens_grad,
        qkv_grad,
        up[:rows].astype(F32),
        up_grad,
        down.astype(F32),
        vec[QB],
        vec[VB],
        vec[OB],
        ubg,
        vec[DBI],
        vec[G1],
        vec[C1],
        vec[G2],
        vec[C2],
    )


def solution(mesh):
    rows = P(("dp", "fsdp"), None)
    mat, vec = P("fsdp", None), P("fsdp")
    return jax.shard_map(
        functools.partial(on_device, mesh.shape["fsdp"], mesh.shape["dp"]),
        mesh=mesh,
        in_specs=(rows, P(("dp", "fsdp")), rows) + (mat,) * 4 + (vec,) * 9,
        out_specs=(rows, rows) + (mat,) * 4 + (vec,) * 9,
        check_vma=False,
    )
```

```python
import functools
import math

import jax
import jax.numpy as jnp
from jax import lax
from jax.experimental import pallas as pl
from jax.experimental.pallas import tpu as pltpu
from jax.sharding import PartitionSpec as P

D = 512
HEADS = 8
HD = 64
FF = 2048
HALF = 512
DB = 128
BIAS = 16
EPS = 1e-05
MASKED = -1e30
F32 = jnp.float32
BF = jnp.bfloat16
LOG2E = math.log2(math.e)
QSCALE = 0.125 * LOG2E
LN2 = math.log(2.0)
CK = math.sqrt(2.0 / math.pi)
CA = 0.044715
NN = (((1,), (0,)), ((), ()))
NT = (((1,), (1,)), ((), ()))
TN = (((0,), (0,)), ((), ()))

SM = pl.BlockSpec(memory_space=pltpu.SMEM)
QB, VB, OB, DBI, G1, C1, G2, C2, UB = range(9)


def mm(a, b, dims):
    return lax.dot_general(a, b, dims, preferred_element_type=F32)


class Copies:
    def __init__(self, sems):
        self.sems, self.used, self.out = sems, 0, []

    def start(self, src, dst):
        copy = pltpu.make_async_copy(src, dst, self.sems.at[self.used])
        self.used += 1
        copy.start()
        return copy

    def send(self, src, dst):
        self.out.append(self.start(src, dst))

    def finish(self):
        for copy in self.out:
            copy.wait()


class Held:
    def __init__(self, copies, src, buf):
        self.buf, self.copies = buf, [copies.start(src, buf)]

    @property
    def ref(self):
        for copy in self.copies:
            copy.wait()
        self.copies = []
        return self.buf


SPECS = {"S": SM, "A": pl.BlockSpec(memory_space=pltpu.HBM), "V": pl.BlockSpec(memory_space=pltpu.VMEM)}


def run(body, ins, outs, bufs=(), sems=64, flops=5 * 10**10, name=None, room=6):
    n_in, n_out = len(ins), len(outs)

    def kernel(*refs):
        copies = Copies(refs[-1])
        body(copies, refs[:n_in], refs[n_in : n_in + n_out], refs[n_in + n_out : -1])
        copies.finish()

    scratch = sum(math.prod(shape) * jnp.dtype(d).itemsize for shape, d in bufs)
    return pl.pallas_call(
        kernel,
        out_shape=[jax.ShapeDtypeStruct(o[0], o[1]) for o in outs],
        in_specs=[SPECS[k] for _, k in ins],
        out_specs=[SPECS[o[2]] for o in outs],
        scratch_shapes=[pltpu.VMEM(shape, d) for shape, d in bufs] + [pltpu.SemaphoreType.DMA((sems,))],
        compiler_params=pltpu.CompilerParams(vmem_limit_bytes=scratch + room * 2**20),
        cost_estimate=pl.CostEstimate(flops=flops, bytes_accessed=1, transcendentals=0),
        name=name,
    )(*ins_only(ins))


def ins_only(ins):
    return [a for a, _ in ins]


def kind(k, *arrays):
    return [(a, k) for a in arrays]


def step_bits(n):
    bits = [1 << p for p in range(1, n.bit_length() - 1)]
    return bits[::-1], bits


def masks(bits):
    k = len(bits)
    found = []
    for s in range(1 << k):
        m = 0
        for p in range(k):
            if not (s >> (k - 1 - p)) & 1:
                m ^= bits[p]
        found.append(m)
    return found


def swap_core(x, n):
    return lax.ppermute(x, "fsdp", [(i, i ^ 1) for i in range(n)])


def swap_step(x, n, p):
    even, odd = step_bits(n)
    return lax.ppermute(x, "fsdp", [(i, i ^ (odd[p] if i & 1 else even[p])) for i in range(n)])


def after(x, *others):
    return lax.optimization_barrier((x,) + others)[0]


def gather_masks(n):
    return list(range(0, n, 2)) + list(range(1, n, 2))


class Gather:
    def __init__(self, x, n):
        self.n = n
        self.have = [x] + [lax.ppermute(x, "fsdp", [(i, i ^ m) for i in range(n)]) for m in range(2, n, 2)]

    def pieces(self, *others):
        return self.have + [swap_core(after(t, *others), self.n) for t in self.have]


def add_parts(parts, rows, last=False):
    total = sum(a[f : f + rows].astype(F32) for a, f in parts)
    return total if last else lax.optimization_barrier(total.astype(BF))


def swap_dp(x, n, d, even, odd):
    pairs = []
    for z in range(d):
        for i in range(n):
            pairs.append((z * n + i, (z ^ (odd if i & 1 else even)) * n + i))
    return lax.ppermute(x, ("dp", "fsdp"), pairs)


def dp_steps(d):
    bits = [1 << p for p in range(d.bit_length() - 1)]
    return list(zip(bits, bits[::-1]))


class Sum:
    def __init__(self, n, d, send, keeps):
        self.n, self.d, self.keeps, self.step = n, d, keeps, 0
        self.got = [(swap_core(send, n), 0)]
        self.own = None
        self.dp = dp_steps(d) if d & (d - 1) == 0 else None

    def advance(self, *others):
        if self.step < len(self.keeps):
            keep = self.keeps[self.step]
            rows = keep.shape[0]
            mine = add_parts([(after(keep, *others), 0)] + self.got, rows)
            self.got = [(a, f + rows) for a, f in self.got]
            if self.step < len(self.keeps) - 1:
                self.got.append((swap_step(mine, self.n, self.step), 0))
            else:
                self.own = mine
                self.send_dp()
        else:
            rows = self.own.shape[0]
            end = self.step == len(self.keeps) + len(self.dp) - 1
            mine = self.own = add_parts([(after(self.own, *others), 0), (self.arrive, 0)], rows, end)
            self.send_dp()
        self.step += 1
        return mine

    def send_dp(self):
        at = self.step - len(self.keeps) + 1
        if self.dp is None:
            self.own = lax.psum(self.own, "dp")
        elif at < len(self.dp):
            self.arrive = swap_dp(self.own, self.n, self.d, *self.dp[at])

    def end(self):
        last = len(self.keeps) + (0 if self.dp is None else len(self.dp))
        while self.step < last:
            self.advance()
        return self.own


def norm_stats(x):
    mu = jnp.mean(x, -1, keepdims=True)
    c = x - mu
    rs = lax.rsqrt(jnp.mean(c * c, -1, keepdims=True) + EPS)
    return c * rs, rs


def softmax_rows(s):
    m = jnp.max(s, 0, keepdims=True)
    e = jnp.exp2(s - m)
    return e.astype(BF), 1.0 / jnp.sum(e, 0, keepdims=True)


def same_block(seg_ref, b):
    row = jnp.broadcast_to(seg_ref[:, b * DB : (b + 1) * DB].astype(F32), (DB, DB))
    return row == row.T


def piece_block(n, r):
    return lax.axis_index("fsdp") ^ gather_masks(n)[r]


def slot_block(n, s):
    me = lax.axis_index("fsdp")
    even, odd = (masks(b) for b in step_bits(n))
    if s < n // 2:
        return me ^ jnp.where((me & 1) == 1, odd[s], even[s])
    s -= n // 2
    return me ^ 1 ^ jnp.where((me & 1) == 1, even[s], odd[s])


def is_big(seg_ref):
    last = seg_ref[:, HALF - 128 : HALF].astype(F32)
    lane = lax.broadcasted_iota(jnp.int32, (1, 128), 1)
    return jnp.max(jnp.where(lane == 127, last, -1.0)) == 0.0


def place(copies, n, pieces, first, rows, buf, col=0):
    started = []
    for r in range(n):
        here = pl.ds(pl.multiple_of(piece_block(n, r) * rows, rows), rows)
        started.append(copies.start(pieces[r].at[pl.ds(first, rows), :], buf.at[here, pl.ds(col, D)]))
    return started


def wait_all(started):
    for copy in started:
        copy.wait()


def pack_body(n, copies, ins, outs, bufs):
    wq, wo, wu = ins[:3]
    vecs = ins[3:]
    a_o, b_o = outs
    rows = wq.shape[0]
    a, b = bufs[:2]
    vbufs = bufs[2:]
    mats = [copies.start(wq.at[:, pl.ds(c * D, D)], a.at[pl.ds(c * rows, rows), :]) for c in range(3)]
    held = [Held(copies, v, vb) for v, vb in zip(vecs, vbufs)]
    rest = [copies.start(wo, b.at[pl.ds(0, rows), :])]
    for c in range(4):
        rest.append(copies.start(wu.at[:, pl.ds(c * D, D)], b.at[pl.ds((1 + c) * rows, rows), :]))
    full = []
    for h in held:
        g = h.ref[...].astype(F32).reshape(1, -1)
        full.append(jnp.concatenate([g] * (D // g.shape[1]), 1))
    full.append(jnp.zeros((BIAS - len(full), D), F32))
    a[pl.ds(3 * rows, BIAS), :] = jnp.concatenate(full, 0).astype(BF)
    wait_all(mats)
    copies.send(a, a_o)
    wait_all(rest)
    copies.send(b, b_o)


def qkv_body(n, rows, copies, ins, outs, bufs):
    x_h = ins[0]
    pieces = ins[1:]
    bias_b, w, h1_b, q, k, v, kt, vt = outs
    x, lines = bufs
    t = x.shape[0]
    x = Held(copies, x_h, x)
    vecs = [copies.start(pieces[r].at[pl.ds(3 * rows, BIAS), :], lines.at[r]) for r in range(n)]
    parts = [place(copies, n, pieces, c * rows, rows, w, c * D) for c in range(3)]
    wait_all(vecs)
    lane = lax.broadcasted_iota(jnp.int32, (BIAS, D), 1)
    bias = jnp.zeros((BIAS, D), F32)
    ub = [jnp.zeros((1, D), F32) for _ in range(4)]
    for r in range(n):
        j = piece_block(n, r)
        got = lines[r].astype(F32)
        bias = jnp.where(lane // (D // n) == j, got, bias)
        for c in range(4):
            ub[c] = jnp.where(c * (n // 4) + lane[:1, :] // (FF // n) == j, got[UB : UB + 1, :], ub[c])
    bias_b[0:BIAS, :] = bias
    for c in range(4):
        bias_b[UB + c : UB + c + 1, :] = ub[c]
    xr = x.ref
    tile = 256
    for i in range(t // tile):
        at = slice(i * tile, (i + 1) * tile)
        nrm, _ = norm_stats(xr[at, :].astype(F32))
        h1_b[at, :] = (nrm * bias[G1 : G1 + 1, :] + bias[C1 : C1 + 1, :]).astype(BF)
    for c, (buf, tbuf) in enumerate(((q, None), (k, kt), (v, vt))):
        wait_all(parts[c])
        for i in range(t // tile):
            at = slice(i * tile, (i + 1) * tile)
            got = mm(h1_b[at, :], w[:, c * D : (c + 1) * D], NN)
            if c == 0:
                got = (got + bias[QB : QB + 1, :]) * QSCALE
            if c == 2:
                got = got + bias[VB : VB + 1, :]
            got = got.astype(BF)
            buf[at, :] = got
            if tbuf is not None:
                tbuf[:, at] = got.T


def attn_body(n, copies, ins, outs, bufs):
    seg, q, k, vt = ins
    ot, linv_b, e_b, ed_b = outs
    t = q.shape[0]
    nh = HALF // DB
    big = is_big(seg)

    def head(h):
        return slice(h * HD, (h + 1) * HD)

    def finish(h, at, e, linv):
        ot[head(h), at] = (mm(vt[head(h), at], e, NN) * linv).astype(BF)
        linv_b[h : h + 1, at] = linv

    def dense():
        at = slice(0, HALF)
        ahead = mm(k[at, head(0)], q[at, head(0)], NT)
        for h in range(HEADS):
            s = ahead
            if h + 1 < HEADS:
                ahead = mm(k[at, head(h + 1)], q[at, head(h + 1)], NT)
            e, linv = softmax_rows(s)
            e_b[h] = e
            finish(h, at, e, linv)

    def diagonal(blocks):
        keys = [(b, h) for b in blocks for h in range(HEADS)]
        at = {b: slice(b * DB, (b + 1) * DB) for b in blocks}
        same = {b: same_block(seg, b) for b in blocks}
        s = [mm(k[at[b], head(h)], q[at[b], head(h)], NT) for b, h in keys]
        r = [softmax_rows(jnp.where(same[b], x, MASKED)) for (b, h), x in zip(keys, s)]
        for (b, h), (e, _) in zip(keys, r):
            if b < nh:
                e_b[h, at[b], :DB] = e
            else:
                ed_b[h, b - nh] = e
        for (b, h), (e, linv) in zip(keys, r):
            finish(h, at[b], e, linv)

    pl.when(big)(dense)

    @pl.when(jnp.logical_not(big))
    def _():
        for b in range(0, nh, 2):
            diagonal((b, b + 1))

    for b in range(nh, t // DB, 2):
        diagonal((b, b + 1))


def send_slots(copies, n, outs, rows, put):
    send_h, keeps = outs[0], outs[1:]
    s = 0
    for ref in list(keeps) + [send_h]:
        for i in range(ref.shape[0] // rows):
            put(slot_block(n, s), s, ref, i * rows)
            s += 1


def mlp_up_body(n, rows, copies, ins, outs, bufs):
    x_h, ot, bias = ins[:3]
    pieces = ins[3:]
    wo, wu, x2, h2, z, gd = outs
    (x,) = bufs
    t = x.shape[0]
    fr = FF // n
    started = place(copies, n, pieces, 0, rows, wo)
    x = Held(copies, x_h, x)
    ups = [place(copies, n, pieces, (1 + c) * rows, rows, wu, c * D) for c in range(4)]
    wait_all(started)
    x = x.ref
    tile = 256
    for i in range(t // tile):
        at = slice(i * tile, (i + 1) * tile)
        x2[at, :] = x[at, :].astype(F32) + mm(ot[:, at], wo[...], TN) + bias[OB : OB + 1, :]
    gain, shift = bias[G2 : G2 + 1, :], bias[C2 : C2 + 1, :]
    for i in range(t // tile):
        at = slice(i * tile, (i + 1) * tile)
        nrm, _ = norm_stats(x2[at, :])
        h2[at, :] = (nrm * gain + shift).astype(BF)
    for c in range(4):
        wait_all(ups[c])
    for i in range(t // tile):
        at = slice(i * tile, (i + 1) * tile)
        for c in range(4):
            cs = slice(c * D, (c + 1) * D)
            v = mm(h2[at, :], wu[:, cs], NN) + bias[UB + c : UB + c + 1, :]
            v2 = v * v
            hh = 0.5 * jnp.tanh(v * (CK + (CK * CA) * v2)) + 0.5
            zz = v * hh
            z[at, cs] = zz.astype(BF)
            gd[at, cs] = (hh + zz * (1.0 - hh) * (2.0 * CK + (6.0 * CK * CA) * v2)).astype(BF)


def mlp_down_body(n, copies, ins, outs, bufs):
    z, gm_h = ins
    gm, acc = bufs
    gm = Held(copies, gm_h, gm)
    copies.send(z, outs[0])
    gm = gm.ref
    fr = FF // n
    per = D // fr
    for c in range(4):
        acc[pl.ds(c * per, per)] = mm(z[:, c * D : (c + 1) * D], gm[...], TN).astype(BF).reshape(per, fr, D)

    def put(j, s, dst, lo):
        dst[lo : lo + fr, :] = acc[j]

    send_slots(copies, n, outs[1:], fr, put)


def mlp_back_body(n, copies, ins, outs, bufs):
    gm_h, gd = ins[:2]
    pieces = ins[2:]
    wd_h, gu, sums = outs
    gm, wd = bufs
    t = gm.shape[0]
    gm = Held(copies, gm_h, gm)
    wds = place(copies, n, pieces, 0, FF // n, wd)
    gm = gm.ref
    wait_all(wds)
    copies.send(wd, wd_h)
    tile = 256
    ubs = [jnp.zeros((1, D), F32) for _ in range(4)]
    dbs = jnp.zeros((1, D), F32)
    for i in range(t // tile):
        at = slice(i * tile, (i + 1) * tile)
        g = gm[at, :]
        dbs += jnp.sum(g.astype(F32), 0, keepdims=True)
        for c in range(4):
            cs = slice(c * D, (c + 1) * D)
            part = (mm(g, wd[cs, :], NT) * gd[at, cs].astype(F32)).astype(BF)
            gu[at, cs] = part
            ubs[c] += jnp.sum(part.astype(F32), 0, keepdims=True)
    sums[...] = jnp.zeros_like(sums)
    sums[DBI : DBI + 1, :] = dbs
    for c in range(4):
        sums[UB + c : UB + c + 1, :] = ubs[c]


def norm_back_body(copies, ins, outs, bufs):
    gu, wu, x2, bias, wo, linv, ot, sums, gm_h = ins
    ga, got, drow, bg = outs
    gm, r2, go = bufs
    t = x2.shape[0]
    gm = Held(copies, gm_h, gm)
    tile = 256
    gain = bias[G2 : G2 + 1, :]
    for i in range(t // tile):
        at = slice(i * tile, (i + 1) * tile)
        r2[at, :] = mm(gu[at, :], wu[...], NT)
    gm = gm.ref
    g2s = c2s = obs = jnp.zeros((1, D), F32)
    for i in range(t // tile):
        at = slice(i * tile, (i + 1) * tile)
        r = r2[at, :]
        nrm, rs = norm_stats(x2[at, :])
        rn = r * nrm
        g2s += jnp.sum(rn, 0, keepdims=True)
        c2s += jnp.sum(r, 0, keepdims=True)
        dn = r * gain
        dv = rs * (dn - jnp.mean(dn, -1, keepdims=True) - nrm * jnp.mean(rn * gain, -1, keepdims=True))
        out = (gm[at, :].astype(F32) + dv).astype(BF)
        ga[at, :] = out
        obs += jnp.sum(out.astype(F32), 0, keepdims=True)
    for i in range(t // tile):
        at = slice(i * tile, (i + 1) * tile)
        go[...] = mm(wo[...], ga[at, :], NT)
        for h in range(HEADS):
            hs = slice(h * HD, (h + 1) * HD)
            gs = (go[hs, :] * linv[h : h + 1, at]).astype(BF)
            got[hs, at] = gs
            drow[h : h + 1, at] = jnp.sum(gs.astype(F32) * ot[hs, at].astype(F32), 0, keepdims=True)
    bg[...] = sums[...]
    bg[OB : OB + 1, :] = obs
    bg[G2 : G2 + 1, :] = g2s
    bg[C2 : C2 + 1, :] = c2s


def mlp_grad_body(n, rows, copies, ins, outs, bufs):
    ot, ga, h2, gu = ins
    acc_up, acc_out = bufs
    acc_out[...] = mm(ot[...], ga[...], NN).astype(BF)

    acc_up[...] = mm(h2[...], gu[...], TN).astype(BF)

    def put(j, s, dst, lo):
        here = pl.ds(pl.multiple_of(j * rows, rows), rows)
        dst[lo : lo + rows, :] = acc_out[here, :]
        for c in range(4):
            dst[lo + (1 + c) * rows : lo + (2 + c) * rows, :] = acc_up[here, c * D : (c + 1) * D]

    send_slots(copies, n, outs, 5 * rows, put)


def head(h):
    return slice(h * HD, (h + 1) * HD)


def back_dense(e, v, got, drow, kt, q, gqt, gk, gv):
    at = slice(0, HALF)
    ahead = mm(v[at, head(0)], got[head(0), at], NN)
    for h in range(HEADS):
        hs, dp = head(h), ahead
        if h + 1 < HEADS:
            ahead = mm(v[at, head(h + 1)], got[head(h + 1), at], NN)
        prob = e[h]
        ds = (prob.astype(F32) * (dp - drow[h : h + 1, at])).astype(BF)
        gqt[hs, at] = (mm(kt[hs, at], ds, NN) * 0.125).astype(BF)
        gk[at, hs] = (mm(ds, q[at, hs], NN) * LN2).astype(BF)
        gv[at, hs] = mm(prob, got[hs, at], NT).astype(BF)


def back_blocks(blocks, prob, v, got, drow, kt, q, gqt, gk, gv):
    keys = [(b, h) for b in blocks for h in range(HEADS)]
    at = {b: slice(b * DB, (b + 1) * DB) for b in blocks}
    dp = [mm(v[at[b], head(h)], got[head(h), at[b]], NN) for b, h in keys]
    pv = [mm(prob(b, h), got[head(h), at[b]], NT) for b, h in keys]
    ds = [
        (prob(b, h).astype(F32) * (x - drow[h : h + 1, at[b]])).astype(BF) for (b, h), x in zip(keys, dp)
    ]
    pq = [mm(kt[head(h), at[b]], x, NN) for (b, h), x in zip(keys, ds)]
    pk = [mm(x, q[at[b], head(h)], NN) for (b, h), x in zip(keys, ds)]
    for i, (b, h) in enumerate(keys):
        gqt[head(h), at[b]] = (pq[i] * 0.125).astype(BF)
        gk[at[b], head(h)] = (pk[i] * LN2).astype(BF)
        gv[at[b], head(h)] = pv[i].astype(BF)


def attn_back_body(n, copies, ins, outs, bufs):
    seg, v, got, drow, e, kt, q = ins
    gqt, gk, gv = outs
    big = is_big(seg)

    @pl.when(big)
    def _():
        back_dense(e, v, got, drow, kt, q, gqt, gk, gv)

    @pl.when(jnp.logical_not(big))
    def _():
        def prob(b, h):
            return e[h, b * DB : (b + 1) * DB, :DB]

        for b in range(0, HALF // DB, 2):
            back_blocks((b, b + 1), prob, v, got, drow, kt, q, gqt, gk, gv)


def qkv_back_body(copies, ins, outs, bufs):
    v, got, drow, ed, kt, q, gqt0, gk0, gv0, wq, x_h, bias, bg = ins
    dv, g, full_b = outs
    x, gqt, gk, gv, r1 = bufs
    x = Held(copies, x_h, x)
    t = x_h.shape[0]
    nb, nh = t // DB, HALF // DB
    for b in range(nh, nb, 2):
        back_blocks((b, b + 1), lambda b, h: ed[h, b - nh], v, got, drow, kt, q, gqt, gk, gv)
    g[:HALF, :D] = gqt0[...].T
    g[HALF:, :D] = gqt[:, HALF:].T
    g[:HALF, D : 2 * D] = gk0[...]
    g[HALF:, D : 2 * D] = gk[HALF:, :]
    g[:HALF, 2 * D :] = gv0[...]
    g[HALF:, 2 * D :] = gv[HALF:, :]

    tile = 256
    x = x.ref
    gain = bias[G1 : G1 + 1, :]
    for i in range(t // tile):
        at = slice(i * tile, (i + 1) * tile)
        r1[at, :] = mm(g[at, :], wq[...], NT)
    g1s = c1s = qbs = vbs = jnp.zeros((1, D), F32)
    for i in range(t // tile):
        at = slice(i * tile, (i + 1) * tile)
        r = r1[at, :]
        nrm, rs = norm_stats(x[at, :].astype(F32))
        rn = r * nrm
        g1s += jnp.sum(rn, 0, keepdims=True)
        c1s += jnp.sum(r, 0, keepdims=True)
        qbs += jnp.sum(g[at, :D].astype(F32), 0, keepdims=True)
        vbs += jnp.sum(g[at, 2 * D :].astype(F32), 0, keepdims=True)
        dn = r * gain
        dv[at, :] = (
            rs * (dn - jnp.mean(dn, -1, keepdims=True) - nrm * jnp.mean(rn * gain, -1, keepdims=True))
        ).astype(BF)
    row = lax.broadcasted_iota(jnp.int32, (BIAS, D), 0)
    full = bg[...]
    for at, val in ((QB, qbs), (VB, vbs), (G1, g1s), (C1, c1s)):
        full = jnp.where(row == at, val, full)
    full_b[...] = full.astype(BF)


def qkv_grad_body(n, rows, copies, ins, outs, bufs):
    h1, g, lines = ins
    (acc,) = bufs
    acc[...] = mm(h1[...], g[...], TN).astype(BF)

    def put(j, s, dst, lo):
        here = pl.ds(pl.multiple_of(j * rows, rows), rows)
        for c in range(3):
            dst[lo + c * rows : lo + (1 + c) * rows, :] = acc[here, c * D : (c + 1) * D]
        dst[lo + 3 * rows : lo + 3 * rows + BIAS, :] = lines[...]

    send_slots(copies, n, outs, 3 * rows + BIAS, put)


def mixed_body(copies, ins, outs, bufs):
    z_h, wd_h, x2, bias, live = ins
    z, wd, mixed = bufs
    t = mixed.shape[0]
    tile = 256
    wd = Held(copies, wd_h, wd)
    zs = [copies.start(z_h.at[pl.ds(i * tile, tile), :], z.at[pl.ds(i * tile, tile), :]) for i in range(t // tile)]
    cols = jnp.broadcast_to(live[...].astype(F32), (128, t)).T
    wd = wd.ref
    for i in range(t // tile):
        at = slice(i * tile, (i + 1) * tile)
        zs[i].wait()
        out = x2[at, :] + mm(z[at, :], wd[...], NN) + bias[DBI : DBI + 1, :]
        mixed[at, :] = jnp.where(cols[at, :1] >= 0, out, 0.0).astype(BF)
        copies.send(mixed.at[pl.ds(i * tile, tile), :], outs[0].at[pl.ds(i * tile, tile), :])


def tokens_body(copies, ins, outs, bufs):
    ga, dv = ins
    (tg,) = bufs
    tile = 256
    for i in range(tg.shape[0] // tile):
        at = slice(i * tile, (i + 1) * tile)
        tg[at, :] = (ga[at, :].astype(F32) + dv[at, :].astype(F32)).astype(BF)
        copies.send(tg.at[pl.ds(i * tile, tile), :], outs[0].at[pl.ds(i * tile, tile), :])


def on_device(n, d, tokens, segments, cotangent, w_qkv, w_out, w_up, w_down, *vectors):
    t = tokens.shape[0]
    rows = w_qkv.shape[0]
    fr = w_down.shape[0]
    nb, nh = t // DB, HALF // DB
    me = lax.axis_index("fsdp")
    qb, vb, ob, ub, db, g1, c1, g2, c2 = vectors
    lines = [qb, vb, ob, db, g1, c1, g2, c2, ub]
    ra, rb, rc = 3 * rows + BIAS, 5 * rows, fr
    pack_a, pack_b = run(
        functools.partial(pack_body, n),
        kind("A", w_qkv, w_out, w_up, *lines),
        [((ra, D), BF, "A"), ((rb, D), BF, "A")],
        [((ra, D), BF), ((rb, D), BF)] + [(a.shape, BF) for a in lines],
        name="pack",
        room=58,
    )
    a = Gather(pack_a, n)
    b = Gather(pack_b, n)
    got_a = a.pieces()
    c = Gather(after(w_down, a.have[1]), n)
    live = (segments >= 0)[:, None]
    gm = jnp.where(live, cotangent, jnp.zeros_like(cotangent))
    seg_row = segments[None, :]

    tok, tokt, wide = ((t, D), BF), ((D, t), BF), ((t, FF), BF)
    hrow, bias_s, tokf = ((HEADS, t), F32), ((BIAS, D), F32), ((t, D), F32)
    bias, wq, h1, q, k, v, kt, vt = run(
        functools.partial(qkv_body, n, rows),
        kind("A", tokens, *got_a),
        [o + ("V",) for o in (bias_s, ((D, 3 * D), BF), tok, tok, tok, tok, tokt, tokt)],
        [tok, ((n, BIAS, D), BF)],
        sems=96,
        name="qkv",
        room=44,
    )
    ot, linv, e, ed = run(
        functools.partial(attn_body, n),
        kind("V", seg_row, q, k, vt),
        [o + ("V",) for o in (tokt, hrow, ((HEADS, HALF, HALF), BF), ((HEADS, nb - nh, DB, DB), BF))],
        name="attn",
    )
    got_b = b.pieces(ot)

    steps = len(step_bits(n)[0])
    counts = [1 << (steps - 1 - p) for p in range(steps)] + [1]

    def slots(r):
        return [((n // 2 * r, D), BF, "V")] + [((m * r, D), BF, "V") for m in counts]

    wo, wu, x2, h2, z, gd = run(
        functools.partial(mlp_up_body, n, rows),
        kind("A", tokens) + kind("V", ot, bias) + kind("A", *got_b),
        [o + ("V",) for o in (((D, D), BF), ((D, FF), BF), tokf, tok, wide, wide)],
        [tok],
        name="mlp_up",
    )
    got_c = c.pieces(h2)
    z_far, *down = run(
        functools.partial(mlp_down_body, n),
        kind("V", z) + kind("A", gm),
        [wide + ("A",)] + slots(rc),
        [tok, ((n, rc, D), BF)],
        name="mlp_down",
    )
    down = Sum(n, d, down[0], down[1:])

    wd, gu, sums = run(
        functools.partial(mlp_back_body, n),
        kind("A", gm) + kind("V", gd) + kind("A", *got_c),
        [((FF, D), BF, "A"), wide + ("V",), bias_s + ("V",)],
        [tok, ((FF, D), BF)],
        name="mlp_back",
    )
    s = down.advance(gu)
    ga, got, drow, bg = run(
        norm_back_body,
        kind("V", after(gu, s), wu, x2, bias, wo, linv, ot, sums) + kind("A", gm),
        [o + ("V",) for o in (tok, tokt, hrow, bias_s)],
        [tok, tokf, ((D, 256), F32)],
        name="norm_back",
    )
    up = run(
        functools.partial(mlp_grad_body, n, rows),
        kind("V", ot, ga, h2, gu),
        slots(rb),
        [((D, FF), BF), ((D, D), BF)],
        name="mlp_grad",
    )
    up_sent = up[0]
    up = Sum(n, d, up[0], up[1:])
    s = down.advance(up_sent)
    half, halft = ((HALF, D), BF), ((D, HALF), BF)
    gqt, gk, gv = run(
        functools.partial(attn_back_body, n),
        kind("V", seg_row, after(v, s), got, drow, e, kt, q),
        [o + ("V",) for o in (halft, half, half)],
        name="attn_back",
    )
    s = down.advance(gk)
    r = up.advance(gk, s)
    dv, g, lines_b = run(
        qkv_back_body,
        kind("V", after(v, s, r), got, drow, ed, kt, q, gqt, gk, gv, wq) + kind("A", tokens) + kind("V", bias, bg),
        [tok + ("V",), ((t, 3 * D), BF, "V"), ((BIAS, D), BF, "V")],
        [tok, tokt, tok, tok, tokf],
        name="qkv_back",
    )
    last = run(
        functools.partial(qkv_grad_body, n, rows),
        kind("V", h1, g, lines_b),
        slots(ra),
        [((D, 3 * D), BF)],
        sems=128,
        name="qkv_grad",
    )
    s = down.advance(last[0])
    last_sent = after(last[0], s)
    last = Sum(n, d, last_sent, last[1:])
    r = up.advance(last_sent)
    r = last.advance(r)
    (mixed,) = run(
        mixed_body,
        kind("A", after(z_far, r), wd) + kind("V", x2, bias, seg_row),
        [tok + ("A",)],
        [wide, ((FF, D), BF), tok],
        name="mixed",
    )
    s = up.advance(mixed)
    s = down.advance(s)
    r = last.advance(s)
    (tokens_grad,) = run(
        tokens_body,
        kind("V", after(ga, r), dv),
        [tok + ("A",)],
        [tok],
        name="tokens",
    )
    r = last.advance(tokens_grad)
    s = up.advance(r)
    r = last.advance(s)
    s = up.advance(r)
    r = last.advance(s)
    down, up, last = down.end(), up.end(), last.end()
    part = D // n
    first = me * part
    vec = lax.dynamic_slice(last, (3 * rows, first), (BIAS, part)).astype(F32)
    ubg = lax.dynamic_slice(last[3 * rows + UB : 3 * rows + UB + 4, :].reshape(-1), (me * fr,), (fr,)).astype(F32)
    qkv_grad = jnp.concatenate([last[c * rows : (c + 1) * rows] for c in range(3)], 1).astype(F32)
    up_grad = jnp.concatenate([up[(1 + c) * rows : (2 + c) * rows] for c in range(4)], 1).astype(F32)
    return (
        mixed,
        tokens_grad,
        qkv_grad,
        up[:rows].astype(F32),
        up_grad,
        down.astype(F32),
        vec[QB],
        vec[VB],
        vec[OB],
        ubg,
        vec[DBI],
        vec[G1],
        vec[C1],
        vec[G2],
        vec[C2],
    )


def solution(mesh):
    rows = P(("dp", "fsdp"), None)
    mat, vec = P("fsdp", None), P("fsdp")
    return jax.shard_map(
        functools.partial(on_device, mesh.shape["fsdp"], mesh.shape["dp"]),
        mesh=mesh,
        in_specs=(rows, P(("dp", "fsdp")), rows) + (mat,) * 4 + (vec,) * 9,
        out_specs=(rows, rows) + (mat,) * 4 + (vec,) * 9,
        check_vma=False,
    )
```

```python
import functools
import math

import jax
import jax.numpy as jnp
from jax import lax
from jax.experimental import pallas as pl
from jax.experimental.pallas import tpu as pltpu
from jax.sharding import PartitionSpec as P

D = 512
HEADS = 8
HD = 64
FF = 2048
HALF = 512
DB = 128
BIAS = 16
EPS = 1e-05
MASKED = -1e30
F32 = jnp.float32
BF = jnp.bfloat16
LOG2E = math.log2(math.e)
QSCALE = 0.125 * LOG2E
LN2 = math.log(2.0)
CK = math.sqrt(2.0 / math.pi)
CA = 0.044715
NN = (((1,), (0,)), ((), ()))
NT = (((1,), (1,)), ((), ()))
TN = (((0,), (0,)), ((), ()))

SM = pl.BlockSpec(memory_space=pltpu.SMEM)
QB, VB, OB, DBI, G1, C1, G2, C2, UB = range(9)


def mm(a, b, dims):
    return lax.dot_general(a, b, dims, preferred_element_type=F32)


class Copies:
    def __init__(self, sems):
        self.sems, self.used, self.out = sems, 0, []

    def start(self, src, dst):
        copy = pltpu.make_async_copy(src, dst, self.sems.at[self.used])
        self.used += 1
        copy.start()
        return copy

    def send(self, src, dst):
        self.out.append(self.start(src, dst))

    def finish(self):
        for copy in self.out:
            copy.wait()


class Held:
    def __init__(self, copies, src, buf):
        self.buf, self.copies = buf, [copies.start(src, buf)]

    @property
    def ref(self):
        for copy in self.copies:
            copy.wait()
        self.copies = []
        return self.buf


SPECS = {"S": SM, "A": pl.BlockSpec(memory_space=pltpu.HBM), "V": pl.BlockSpec(memory_space=pltpu.VMEM)}


def run(body, ins, outs, bufs=(), sems=64, flops=5 * 10**10, name=None, room=6, alias=None):
    n_in, n_out = len(ins), len(outs)

    def kernel(*refs):
        copies = Copies(refs[-1])
        body(copies, refs[:n_in], refs[n_in : n_in + n_out], refs[n_in + n_out : -1])
        copies.finish()

    scratch = sum(math.prod(shape) * jnp.dtype(d).itemsize for shape, d in bufs)
    return pl.pallas_call(
        kernel,
        out_shape=[jax.ShapeDtypeStruct(o[0], o[1]) for o in outs],
        in_specs=[SPECS[k] for _, k in ins],
        out_specs=[SPECS[o[2]] for o in outs],
        scratch_shapes=[pltpu.VMEM(shape, d) for shape, d in bufs] + [pltpu.SemaphoreType.DMA((sems,))],
        compiler_params=pltpu.CompilerParams(vmem_limit_bytes=scratch + room * 2**20),
        cost_estimate=pl.CostEstimate(flops=flops, bytes_accessed=1, transcendentals=0),
        name=name,
        input_output_aliases=alias or {},
    )(*ins_only(ins))


def ins_only(ins):
    return [a for a, _ in ins]


def kind(k, *arrays):
    return [(a, k) for a in arrays]


def step_bits(n):
    bits = [1 << p for p in range(1, n.bit_length() - 1)]
    return bits[::-1], bits


def masks(bits):
    k = len(bits)
    found = []
    for s in range(1 << k):
        m = 0
        for p in range(k):
            if not (s >> (k - 1 - p)) & 1:
                m ^= bits[p]
        found.append(m)
    return found


def swap_core(x, n):
    return lax.ppermute(x, "fsdp", [(i, i ^ 1) for i in range(n)])


def swap_step(x, n, p):
    even, odd = step_bits(n)
    return lax.ppermute(x, "fsdp", [(i, i ^ (odd[p] if i & 1 else even[p])) for i in range(n)])


def after(x, *others):
    return lax.optimization_barrier((x,) + others)[0]


def gather_masks(n):
    return list(range(0, n, 2)) + list(range(1, n, 2))


class Gather:
    def __init__(self, x, n):
        self.n = n
        self.have = [x] + [lax.ppermute(x, "fsdp", [(i, i ^ m) for i in range(n)]) for m in range(2, n, 2)]

    def pieces(self, *others):
        return self.have + [swap_core(after(t, *others), self.n) for t in self.have]


def add_parts(parts, rows, last=False):
    total = sum(a[f : f + rows].astype(F32) for a, f in parts)
    return total if last else lax.optimization_barrier(total.astype(BF))


def swap_dp(x, n, d, even, odd):
    pairs = []
    for z in range(d):
        for i in range(n):
            pairs.append((z * n + i, (z ^ (odd if i & 1 else even)) * n + i))
    return lax.ppermute(x, ("dp", "fsdp"), pairs)


def dp_steps(d):
    bits = [1 << p for p in range(d.bit_length() - 1)]
    return list(zip(bits, bits[::-1]))


class Sum:
    def __init__(self, n, d, send, keeps):
        self.n, self.d, self.keeps, self.step = n, d, keeps, 0
        self.got = [(swap_core(send, n), 0)]
        self.own = None
        self.dp = dp_steps(d) if d & (d - 1) == 0 else None

    def advance(self, *others, send=True):
        if self.step < len(self.keeps):
            keep = self.keeps[self.step]
            rows = keep.shape[0]
            mine = add_parts([(after(keep, *others), 0)] + self.got, rows)
            self.got = [(a, f + rows) for a, f in self.got]
            if self.step < len(self.keeps) - 1:
                self.got.append((swap_step(mine, self.n, self.step), 0))
            else:
                self.own = mine
                self.send_dp()
        else:
            rows = self.own.shape[0]
            end = self.step == len(self.keeps) + len(self.dp) - 1
            mine = self.own = add_parts([(after(self.own, *others), 0), (self.arrive, 0)], rows, end)
            if send:
                self.send_dp()
        self.step += 1
        return mine

    def send_later(self, *others):
        self.step -= 1
        self.send_dp(*others)
        self.step += 1

    def send_dp(self, *others):
        at = self.step - len(self.keeps) + 1
        if self.dp is None:
            self.own = lax.psum(self.own, "dp")
        elif at < len(self.dp):
            self.arrive = swap_dp(after(self.own, *others), self.n, self.d, *self.dp[at])

    def end(self):
        last = len(self.keeps) + (0 if self.dp is None else len(self.dp))
        while self.step < last:
            self.advance()
        return self.own


def staggered(keys, product, use):
    ahead = product(*keys[0])
    for i, key in enumerate(keys):
        now = ahead
        if i + 1 < len(keys):
            ahead = product(*keys[i + 1])
        use(*key, now)


def norm_stats(x):
    mu = jnp.mean(x, -1, keepdims=True)
    c = x - mu
    rs = lax.rsqrt(jnp.mean(c * c, -1, keepdims=True) + EPS)
    return c * rs, rs


def softmax_rows(s):
    m = jnp.max(s, 0, keepdims=True)
    e = jnp.exp2(s - m)
    return e.astype(BF), 1.0 / jnp.sum(e, 0, keepdims=True)


def same_block(seg_ref, b):
    row = jnp.broadcast_to(seg_ref[:, b * DB : (b + 1) * DB].astype(F32), (DB, DB))
    return row == row.T


def piece_block(n, r):
    return lax.axis_index("fsdp") ^ gather_masks(n)[r]


def slot_block(n, s):
    me = lax.axis_index("fsdp")
    even, odd = (masks(b) for b in step_bits(n))
    if s < n // 2:
        return me ^ jnp.where((me & 1) == 1, odd[s], even[s])
    s -= n // 2
    return me ^ 1 ^ jnp.where((me & 1) == 1, even[s], odd[s])


def is_big(seg_ref):
    last = seg_ref[:, HALF - 128 : HALF].astype(F32)
    lane = lax.broadcasted_iota(jnp.int32, (1, 128), 1)
    return jnp.max(jnp.where(lane == 127, last, -1.0)) == 0.0


def place(copies, n, pieces, first, rows, buf, col=0):
    started = []
    for r in range(n):
        here = pl.ds(pl.multiple_of(piece_block(n, r) * rows, rows), rows)
        started.append(copies.start(pieces[r].at[pl.ds(first, rows), :], buf.at[here, pl.ds(col, D)]))
    return started


def wait_all(started):
    for copy in started:
        copy.wait()


def pack_body(n, copies, ins, outs, bufs):
    wq, wo, wu = ins[:3]
    vecs = ins[3:]
    a_o, b_o = outs
    rows = wq.shape[0]
    a, b = bufs[:2]
    vbufs = bufs[2:]
    mats = [copies.start(wq.at[:, pl.ds(c * D, D)], a.at[pl.ds(c * rows, rows), :]) for c in range(3)]
    held = [Held(copies, v, vb) for v, vb in zip(vecs, vbufs)]
    rest = [copies.start(wo, b.at[pl.ds(0, rows), :])]
    for c in range(4):
        rest.append(copies.start(wu.at[:, pl.ds(c * D, D)], b.at[pl.ds((1 + c) * rows, rows), :]))
    full = []
    for h in held:
        g = h.ref[...].astype(F32).reshape(1, -1)
        full.append(jnp.concatenate([g] * (D // g.shape[1]), 1))
    full.append(jnp.zeros((BIAS - len(full), D), F32))
    a[pl.ds(3 * rows, BIAS), :] = jnp.concatenate(full, 0).astype(BF)
    wait_all(mats)
    copies.send(a, a_o)
    wait_all(rest)
    copies.send(b, b_o)


def qkv_body(n, rows, copies, ins, outs, bufs):
    x_h = ins[0]
    pieces = ins[1:]
    bias_b, w, h1_b, q, k, v, kt, vt = outs
    x, lines = bufs
    t = x.shape[0]
    x = Held(copies, x_h, x)
    vecs = [copies.start(pieces[r].at[pl.ds(3 * rows, BIAS), :], lines.at[r]) for r in range(n)]
    parts = [place(copies, n, pieces, c * rows, rows, w, c * D) for c in range(3)]
    wait_all(vecs)
    lane = lax.broadcasted_iota(jnp.int32, (BIAS, D), 1)
    bias = jnp.zeros((BIAS, D), F32)
    ub = [jnp.zeros((1, D), F32) for _ in range(4)]
    for r in range(n):
        j = piece_block(n, r)
        got = lines[r].astype(F32)
        bias = jnp.where(lane // (D // n) == j, got, bias)
        for c in range(4):
            ub[c] = jnp.where(c * (n // 4) + lane[:1, :] // (FF // n) == j, got[UB : UB + 1, :], ub[c])
    bias_b[0:BIAS, :] = bias
    for c in range(4):
        bias_b[UB + c : UB + c + 1, :] = ub[c]
    xr = x.ref
    tile = 256
    for started in parts:
        wait_all(started)

    def norm(at):
        nrm, _ = norm_stats(xr[at, :].astype(F32))
        h1 = (nrm * bias[G1 : G1 + 1, :] + bias[C1 : C1 + 1, :]).astype(BF)
        h1_b[at, :] = h1
        return h1

    def project(at, h1):
        q[at, :] = ((mm(h1, w[:, :D], NN) + bias[QB : QB + 1, :]) * QSCALE).astype(BF)
        kk = mm(h1, w[:, D : 2 * D], NN).astype(BF)
        k[at, :] = kk
        kt[:, at] = kk.T
        vv = (mm(h1, w[:, 2 * D :], NN) + bias[VB : VB + 1, :]).astype(BF)
        v[at, :] = vv
        vt[:, at] = vv.T

    staggered([(slice(i * tile, (i + 1) * tile),) for i in range(t // tile)], norm, project)


def attn_body(n, copies, ins, outs, bufs):
    seg, q, k, vt = ins
    ot, linv_b, e_b, ed_b = outs
    t = q.shape[0]
    nh = HALF // DB
    big = is_big(seg)

    def head(h):
        return slice(h * HD, (h + 1) * HD)

    def finish(h, at, e, linv):
        ot[head(h), at] = (mm(vt[head(h), at], e, NN) * linv).astype(BF)
        linv_b[h : h + 1, at] = linv

    def dense():
        at = slice(0, HALF)
        ahead = mm(k[at, head(0)], q[at, head(0)], NT)
        for h in range(HEADS):
            s = ahead
            if h + 1 < HEADS:
                ahead = mm(k[at, head(h + 1)], q[at, head(h + 1)], NT)
            e, linv = softmax_rows(s)
            e_b[h] = e
            finish(h, at, e, linv)

    def diagonal(blocks):
        keys = [(b, h) for b in blocks for h in range(HEADS)]
        at = {b: slice(b * DB, (b + 1) * DB) for b in blocks}
        same = {b: same_block(seg, b) for b in blocks}
        s = [mm(k[at[b], head(h)], q[at[b], head(h)], NT) for b, h in keys]
        r = [softmax_rows(jnp.where(same[b], x, MASKED)) for (b, h), x in zip(keys, s)]
        for (b, h), (e, _) in zip(keys, r):
            if b < nh:
                e_b[h, at[b], :DB] = e
            else:
                ed_b[h, b - nh] = e
        for (b, h), (e, linv) in zip(keys, r):
            finish(h, at[b], e, linv)

    pl.when(big)(dense)

    @pl.when(jnp.logical_not(big))
    def _():
        for b in range(0, nh, 2):
            diagonal((b, b + 1))

    for b in range(nh, t // DB, 2):
        diagonal((b, b + 1))


def send_slots(copies, n, outs, rows, put):
    send_h, keeps = outs[0], outs[1:]
    s = 0
    for ref in list(keeps) + [send_h]:
        for i in range(ref.shape[0] // rows):
            put(slot_block(n, s), s, ref, i * rows)
            s += 1


def mlp_up_body(n, rows, copies, ins, outs, bufs):
    x_h, ot, bias = ins[:3]
    pieces = ins[3:]
    wo, wu, x2, h2, z, gd = outs
    (x,) = bufs
    t = x.shape[0]
    fr = FF // n
    started = place(copies, n, pieces, 0, rows, wo)
    x = Held(copies, x_h, x)
    ups = [place(copies, n, pieces, (1 + c) * rows, rows, wu, c * D) for c in range(4)]
    wait_all(started)
    x = x.ref
    tile = 256
    rows_at = [slice(i * tile, (i + 1) * tile) for i in range(t // tile)]
    gain, shift = bias[G2 : G2 + 1, :], bias[C2 : C2 + 1, :]

    def branch(at):
        return mm(ot[:, at], wo[...], TN)

    def norm(at, got):
        v = x[at, :].astype(F32) + got + bias[OB : OB + 1, :]
        x2[at, :] = v
        nrm, _ = norm_stats(v)
        h2[at, :] = (nrm * gain + shift).astype(BF)

    staggered([(at,) for at in rows_at], branch, norm)
    for c in range(4):
        wait_all(ups[c])

    def hidden(at, c):
        return mm(h2[at, :], wu[:, c * D : (c + 1) * D], NN)

    def act(at, c, got):
        cs = slice(c * D, (c + 1) * D)
        v = got + bias[UB + c : UB + c + 1, :]
        v2 = v * v
        hh = 0.5 * jnp.tanh(v * (CK + (CK * CA) * v2)) + 0.5
        zz = v * hh
        z[at, cs] = zz.astype(BF)
        gd[at, cs] = (hh + zz * (1.0 - hh) * (2.0 * CK + (6.0 * CK * CA) * v2)).astype(BF)

    staggered([(at, c) for at in rows_at for c in range(4)], hidden, act)


def mlp_down_body(n, copies, ins, outs, bufs):
    z, x2, gm_h = ins
    gm, acc = bufs
    gm = Held(copies, gm_h, gm)
    copies.send(z, outs[0])
    copies.send(x2, outs[1])
    gm = gm.ref
    fr = FF // n
    per = D // fr
    for c in range(4):
        acc[pl.ds(c * per, per)] = mm(z[:, c * D : (c + 1) * D], gm[...], TN).astype(BF).reshape(per, fr, D)

    def put(j, s, dst, lo):
        dst[lo : lo + fr, :] = acc[j]

    send_slots(copies, n, outs[2:], fr, put)


def mlp_back_body(n, copies, ins, outs, bufs):
    gm_h, gd = ins[:2]
    pieces = ins[2:]
    wd_h, gu, sums = outs
    gm, wd = bufs
    t = gm.shape[0]
    gm = Held(copies, gm_h, gm)
    wds = place(copies, n, pieces, 0, FF // n, wd)
    gm = gm.ref
    wait_all(wds)
    copies.send(wd, wd_h)
    tile = 256
    ubs = [jnp.zeros((1, D), F32) for _ in range(4)]
    dbs = jnp.zeros((1, D), F32)
    rows_at = [slice(i * tile, (i + 1) * tile) for i in range(t // tile)]

    def product(at, c):
        return mm(gm[at, :], wd[c * D : (c + 1) * D, :], NT)

    def use(at, c, got):
        cs = slice(c * D, (c + 1) * D)
        part = (got * gd[at, cs].astype(F32)).astype(BF)
        gu[at, cs] = part
        ubs[c] += jnp.sum(part.astype(F32), 0, keepdims=True)

    staggered([(at, c) for at in rows_at for c in range(4)], product, use)
    for at in rows_at:
        dbs += jnp.sum(gm[at, :].astype(F32), 0, keepdims=True)
    sums[...] = jnp.zeros_like(sums)
    sums[DBI : DBI + 1, :] = dbs
    for c in range(4):
        sums[UB + c : UB + c + 1, :] = ubs[c]


def norm_back_body(copies, ins, outs, bufs):
    gu, wu, x2, bias, wo, linv, ot, sums, gm_h = ins
    ga, got, drow, bg = outs
    (gm,) = bufs
    t = x2.shape[0]
    gm = Held(copies, gm_h, gm)
    tile = 256
    gain = bias[G2 : G2 + 1, :]
    gm = gm.ref
    rows_at = [slice(i * tile, (i + 1) * tile) for i in range(t // tile)]
    total = [jnp.zeros((1, D), F32) for _ in range(3)]

    def back(at):
        return mm(gu[at, :], wu[...], NT)

    def norm(at, r):
        nrm, rs = norm_stats(x2[at, :])
        rn = r * nrm
        total[0] += jnp.sum(rn, 0, keepdims=True)
        total[1] += jnp.sum(r, 0, keepdims=True)
        dn = r * gain
        dv = rs * (dn - jnp.mean(dn, -1, keepdims=True) - nrm * jnp.mean(rn * gain, -1, keepdims=True))
        out = (gm[at, :].astype(F32) + dv).astype(BF)
        ga[at, :] = out
        total[2] += jnp.sum(out.astype(F32), 0, keepdims=True)

    staggered([(at,) for at in rows_at], back, norm)
    g2s, c2s, obs = total

    def product(at):
        return mm(wo[...], ga[at, :], NT)

    def use(at, got_f):
        for h in range(HEADS):
            hs = slice(h * HD, (h + 1) * HD)
            gs = (got_f[hs, :] * linv[h : h + 1, at]).astype(BF)
            got[hs, at] = gs
            drow[h : h + 1, at] = jnp.sum(gs.astype(F32) * ot[hs, at].astype(F32), 0, keepdims=True)

    staggered([(at,) for at in rows_at], product, use)
    bg[...] = sums[...]
    bg[OB : OB + 1, :] = obs
    bg[G2 : G2 + 1, :] = g2s
    bg[C2 : C2 + 1, :] = c2s


def mlp_grad_body(n, rows, copies, ins, outs, bufs):
    ot, ga, h2, gu = ins
    acc_up, acc_out = bufs
    acc_out[...] = mm(ot[...], ga[...], NN).astype(BF)

    acc_up[...] = mm(h2[...], gu[...], TN).astype(BF)

    def put(j, s, dst, lo):
        here = pl.ds(pl.multiple_of(j * rows, rows), rows)
        dst[lo : lo + rows, :] = acc_out[here, :]
        for c in range(4):
            dst[lo + (1 + c) * rows : lo + (2 + c) * rows, :] = acc_up[here, c * D : (c + 1) * D]

    send_slots(copies, n, outs, 5 * rows, put)


def head(h):
    return slice(h * HD, (h + 1) * HD)


def back_dense(e, v, got, drow, kt, q, gqt, gk, gv):
    at = slice(0, HALF)
    ahead = mm(v[at, head(0)], got[head(0), at], NN)
    for h in range(HEADS):
        hs, dp = head(h), ahead
        if h + 1 < HEADS:
            ahead = mm(v[at, head(h + 1)], got[head(h + 1), at], NN)
        prob = e[h]
        ds = (prob.astype(F32) * (dp - drow[h : h + 1, at])).astype(BF)
        gqt[hs, at] = (mm(kt[hs, at], ds, NN) * 0.125).astype(BF)
        gk[at, hs] = (mm(ds, q[at, hs], NN) * LN2).astype(BF)
        gv[at, hs] = mm(prob, got[hs, at], NT).astype(BF)


def back_blocks(blocks, prob, v, got, drow, kt, q, gqt, gk, gv):
    keys = [(b, h) for b in blocks for h in range(HEADS)]
    at = {b: slice(b * DB, (b + 1) * DB) for b in blocks}
    dp = [mm(v[at[b], head(h)], got[head(h), at[b]], NN) for b, h in keys]
    pv = [mm(prob(b, h), got[head(h), at[b]], NT) for b, h in keys]
    ds = [
        (prob(b, h).astype(F32) * (x - drow[h : h + 1, at[b]])).astype(BF) for (b, h), x in zip(keys, dp)
    ]
    pq = [mm(kt[head(h), at[b]], x, NN) for (b, h), x in zip(keys, ds)]
    pk = [mm(x, q[at[b], head(h)], NN) for (b, h), x in zip(keys, ds)]
    for i, (b, h) in enumerate(keys):
        gqt[head(h), at[b]] = (pq[i] * 0.125).astype(BF)
        gk[at[b], head(h)] = (pk[i] * LN2).astype(BF)
        gv[at[b], head(h)] = pv[i].astype(BF)


def attn_back_body(n, copies, ins, outs, bufs):
    seg, v, got, drow, e, kt, q = ins
    gqt, gk, gv = outs
    big = is_big(seg)

    @pl.when(big)
    def _():
        back_dense(e, v, got, drow, kt, q, gqt, gk, gv)

    @pl.when(jnp.logical_not(big))
    def _():
        def prob(b, h):
            return e[h, b * DB : (b + 1) * DB, :DB]

        for b in range(0, HALF // DB, 2):
            back_blocks((b, b + 1), prob, v, got, drow, kt, q, gqt, gk, gv)


def qkv_back_body(copies, ins, outs, bufs):
    v, got, drow, ed, kt, q, gqt0, gk0, gv0, wq, ga, x_h, bias, bg = ins
    tg_h, g, full_b = outs
    x, gqt, gk, gv, tg = bufs
    x = Held(copies, x_h, x)
    t = x_h.shape[0]
    nb, nh = t // DB, HALF // DB
    for b in range(nh, nb, 2):
        back_blocks((b, b + 1), lambda b, h: ed[h, b - nh], v, got, drow, kt, q, gqt, gk, gv)
    g[:HALF, :D] = gqt0[...].T
    g[HALF:, :D] = gqt[:, HALF:].T
    g[:HALF, D : 2 * D] = gk0[...]
    g[HALF:, D : 2 * D] = gk[HALF:, :]
    g[:HALF, 2 * D :] = gv0[...]
    g[HALF:, 2 * D :] = gv[HALF:, :]

    tile = 256
    x = x.ref
    gain = bias[G1 : G1 + 1, :]
    rows_at = [slice(i * tile, (i + 1) * tile) for i in range(t // tile)]
    total = [jnp.zeros((1, D), F32) for _ in range(4)]

    def back(at):
        return mm(g[at, :], wq[...], NT)

    def norm(at, r):
        nrm, rs = norm_stats(x[at, :].astype(F32))
        rn = r * nrm
        total[0] += jnp.sum(rn, 0, keepdims=True)
        total[1] += jnp.sum(r, 0, keepdims=True)
        total[2] += jnp.sum(g[at, :D].astype(F32), 0, keepdims=True)
        total[3] += jnp.sum(g[at, 2 * D :].astype(F32), 0, keepdims=True)
        dn = r * gain
        dv = rs * (dn - jnp.mean(dn, -1, keepdims=True) - nrm * jnp.mean(rn * gain, -1, keepdims=True))
        tg[at, :] = (ga[at, :].astype(F32) + dv).astype(BF)
        copies.send(tg.at[at, :], tg_h.at[at, :])

    staggered([(at,) for at in rows_at], back, norm)
    g1s, c1s, qbs, vbs = total
    row = lax.broadcasted_iota(jnp.int32, (BIAS, D), 0)
    full = bg[...]
    for at, val in ((QB, qbs), (VB, vbs), (G1, g1s), (C1, c1s)):
        full = jnp.where(row == at, val, full)
    full_b[...] = full.astype(BF)


def qkv_grad_body(n, rows, copies, ins, outs, bufs):
    h1, g, lines = ins
    (acc,) = bufs
    acc[...] = mm(h1[...], g[...], TN).astype(BF)

    def put(j, s, dst, lo):
        here = pl.ds(pl.multiple_of(j * rows, rows), rows)
        for c in range(3):
            dst[lo + c * rows : lo + (1 + c) * rows, :] = acc[here, c * D : (c + 1) * D]
        dst[lo + 3 * rows : lo + 3 * rows + BIAS, :] = lines[...]

    send_slots(copies, n, outs, 3 * rows + BIAS, put)


def mixed_body(first, copies, ins, outs, bufs):
    z_h, wd_h, x2_h, bias, live = ins[:5]
    z, wd, x2, mixed = bufs
    t = mixed.shape[0]
    tile = 256
    wd, x2 = Held(copies, wd_h, wd), Held(copies, x2_h.at[pl.ds(first, t), :], x2)
    zs = [
        copies.start(z_h.at[pl.ds(first + i * tile, tile), :], z.at[pl.ds(i * tile, tile), :]) for i in range(t // tile)
    ]
    cols = jnp.broadcast_to(live[:, first : first + t].astype(F32), (128, t)).T
    wd, x2 = wd.ref, x2.ref

    def product(i):
        zs[i].wait()
        return mm(z[i * tile : (i + 1) * tile, :], wd[...], NN)

    def use(i, got):
        at = slice(i * tile, (i + 1) * tile)
        out = x2[at, :] + got + bias[DBI : DBI + 1, :]
        mixed[at, :] = jnp.where(cols[at, :1] >= 0, out, 0.0).astype(BF)
        copies.send(mixed.at[pl.ds(i * tile, tile), :], outs[0].at[pl.ds(first + i * tile, tile), :])

    staggered([(i,) for i in range(t // tile)], product, use)


def on_device(n, d, tokens, segments, cotangent, w_qkv, w_out, w_up, w_down, *vectors):
    t = tokens.shape[0]
    rows = w_qkv.shape[0]
    fr = w_down.shape[0]
    nb, nh = t // DB, HALF // DB
    me = lax.axis_index("fsdp")
    qb, vb, ob, ub, db, g1, c1, g2, c2 = vectors
    lines = [qb, vb, ob, db, g1, c1, g2, c2, ub]
    ra, rb, rc = 3 * rows + BIAS, 5 * rows, fr
    pack_a, pack_b = run(
        functools.partial(pack_body, n),
        kind("A", w_qkv, w_out, w_up, *lines),
        [((ra, D), BF, "A"), ((rb, D), BF, "A")],
        [((ra, D), BF), ((rb, D), BF)] + [(a.shape, BF) for a in lines],
        name="pack",
        room=58,
    )
    a = Gather(pack_a, n)
    b = Gather(pack_b, n)
    got_a = a.pieces()
    c = Gather(after(w_down, a.have[1]), n)
    live = (segments >= 0)[:, None]
    gm = jnp.where(live, cotangent, jnp.zeros_like(cotangent))
    seg_row = segments[None, :]

    tok, tokt, wide = ((t, D), BF), ((D, t), BF), ((t, FF), BF)
    hrow, bias_s, tokf = ((HEADS, t), F32), ((BIAS, D), F32), ((t, D), F32)
    bias, wq, h1, q, k, v, kt, vt = run(
        functools.partial(qkv_body, n, rows),
        kind("A", tokens, *got_a),
        [o + ("V",) for o in (bias_s, ((D, 3 * D), BF), tok, tok, tok, tok, tokt, tokt)],
        [tok, ((n, BIAS, D), BF)],
        sems=96,
        name="qkv",
        room=44,
    )
    ot, linv, e, ed = run(
        functools.partial(attn_body, n),
        kind("V", seg_row, q, k, vt),
        [o + ("V",) for o in (tokt, hrow, ((HEADS, HALF, HALF), BF), ((HEADS, nb - nh, DB, DB), BF))],
        name="attn",
    )
    got_b = b.pieces(ot)

    steps = len(step_bits(n)[0])
    counts = [1 << (steps - 1 - p) for p in range(steps)] + [1]

    def slots(r):
        return [((n // 2 * r, D), BF, "V")] + [((m * r, D), BF, "V") for m in counts]

    wo, wu, x2, h2, z, gd = run(
        functools.partial(mlp_up_body, n, rows),
        kind("A", tokens) + kind("V", ot, bias) + kind("A", *got_b),
        [o + ("V",) for o in (((D, D), BF), ((D, FF), BF), tokf, tok, wide, wide)],
        [tok],
        name="mlp_up",
    )
    got_c = c.pieces(h2)
    z_far, x2_far, *down = run(
        functools.partial(mlp_down_body, n),
        kind("V", z, x2) + kind("A", gm),
        [wide + ("A",), tokf + ("A",)] + slots(rc),
        [tok, ((n, rc, D), BF)],
        name="mlp_down",
    )
    down = Sum(n, d, down[0], down[1:])

    wd, gu, sums = run(
        functools.partial(mlp_back_body, n),
        kind("A", gm) + kind("V", gd) + kind("A", *got_c),
        [((FF, D), BF, "A"), wide + ("V",), bias_s + ("V",)],
        [tok, ((FF, D), BF)],
        name="mlp_back",
    )
    s = down.advance(gu)
    ga, got, drow, bg = run(
        norm_back_body,
        kind("V", after(gu, s), wu, x2, bias, wo, linv, ot, sums) + kind("A", gm),
        [o + ("V",) for o in (tok, tokt, hrow, bias_s)],
        [tok],
        name="norm_back",
    )
    up = run(
        functools.partial(mlp_grad_body, n, rows),
        kind("V", ot, ga, h2, gu),
        slots(rb),
        [((D, FF), BF), ((D, D), BF)],
        name="mlp_grad",
    )
    up_sent = up[0]
    up = Sum(n, d, up[0], up[1:])
    s = down.advance(up_sent)
    half, halft = ((HALF, D), BF), ((D, HALF), BF)
    gqt, gk, gv = run(
        functools.partial(attn_back_body, n),
        kind("V", seg_row, after(v, s), got, drow, e, kt, q),
        [o + ("V",) for o in (halft, half, half)],
        name="attn_back",
    )
    r = up.advance(gk)
    s = down.advance(gk, r)
    tokens_grad, g, lines_b = run(
        qkv_back_body,
        kind("V", after(v, s, r), got, drow, ed, kt, q, gqt, gk, gv, wq, ga) + kind("A", tokens) + kind("V", bias, bg),
        [tok + ("A",), ((t, 3 * D), BF, "V"), ((BIAS, D), BF, "V")],
        [tok, tokt, tok, tok, tok],
        name="qkv_back",
    )
    last = run(
        functools.partial(qkv_grad_body, n, rows),
        kind("V", h1, g, lines_b),
        slots(ra),
        [((D, 3 * D), BF)],
        sems=128,
        name="qkv_grad",
    )
    s = down.advance(last[0], send=False)
    last_sent = after(last[0], s)
    last = Sum(n, d, last_sent, last[1:])
    r = up.advance(last_sent)
    down.send_later(r)
    r = last.advance(r)
    def half_mixed(part, hold, *before):
        (out,) = run(
            functools.partial(mixed_body, part * (t // 2)),
            kind("A", after(z_far, hold), wd, x2_far) + kind("V", bias, seg_row) + kind("A", *before),
            [tok + ("A",)],
            [((t // 2, FF), BF), ((FF, D), BF), ((t // 2, D), F32), ((t // 2, D), BF)],
            name="mixed" + str(part),
            alias={5: 0} if before else None,
        )
        return out

    mixed = half_mixed(0, r)
    s = up.advance(mixed)
    r = last.advance(s)
    mixed = half_mixed(1, r, mixed)
    s = down.advance(mixed)
    r = last.advance(s)
    s = up.advance(r)
    r = last.advance(s)
    s = up.advance(r)
    r = last.advance(s)
    down, up, last = down.end(), up.end(), last.end()
    part = D // n
    first = me * part
    vec = lax.dynamic_slice(last, (3 * rows, first), (BIAS, part)).astype(F32)
    ubg = lax.dynamic_slice(last[3 * rows + UB : 3 * rows + UB + 4, :].reshape(-1), (me * fr,), (fr,)).astype(F32)
    qkv_grad = jnp.concatenate([last[c * rows : (c + 1) * rows] for c in range(3)], 1).astype(F32)
    up_grad = jnp.concatenate([up[(1 + c) * rows : (2 + c) * rows] for c in range(4)], 1).astype(F32)
    return (
        mixed,
        tokens_grad,
        qkv_grad,
        up[:rows].astype(F32),
        up_grad,
        down.astype(F32),
        vec[QB],
        vec[VB],
        vec[OB],
        ubg,
        vec[DBI],
        vec[G1],
        vec[C1],
        vec[G2],
        vec[C2],
    )


def solution(mesh):
    rows = P(("dp", "fsdp"), None)
    mat, vec = P("fsdp", None), P("fsdp")
    return jax.shard_map(
        functools.partial(on_device, mesh.shape["fsdp"], mesh.shape["dp"]),
        mesh=mesh,
        in_specs=(rows, P(("dp", "fsdp")), rows) + (mat,) * 4 + (vec,) * 9,
        out_specs=(rows, rows) + (mat,) * 4 + (vec,) * 9,
        check_vma=False,
    )
```

```python
import functools
import math

import jax
import jax.numpy as jnp
from jax import lax
from jax.experimental import pallas as pl
from jax.experimental.pallas import tpu as pltpu
from jax.sharding import PartitionSpec as P

D = 512
HEADS = 8
HD = 64
FF = 2048
HALF = 512
DB = 128
BIAS = 16
EPS = 1e-05
MASKED = -1e30
F32 = jnp.float32
BF = jnp.bfloat16
LOG2E = math.log2(math.e)
QSCALE = 0.125 * LOG2E
LN2 = math.log(2.0)
CK = math.sqrt(2.0 / math.pi)
CA = 0.044715
NN = (((1,), (0,)), ((), ()))
NT = (((1,), (1,)), ((), ()))
TN = (((0,), (0,)), ((), ()))

SM = pl.BlockSpec(memory_space=pltpu.SMEM)
QB, VB, OB, DBI, G1, C1, G2, C2, UB = range(9)


def mm(a, b, dims):
    return lax.dot_general(a, b, dims, preferred_element_type=F32)


class Copies:
    def __init__(self, sems):
        self.sems, self.used, self.out = sems, 0, []

    def start(self, src, dst):
        copy = pltpu.make_async_copy(src, dst, self.sems.at[self.used])
        self.used += 1
        copy.start()
        return copy

    def send(self, src, dst):
        self.out.append(self.start(src, dst))

    def finish(self):
        for copy in self.out:
            copy.wait()


class Held:
    def __init__(self, copies, src, buf):
        self.buf, self.copies = buf, [copies.start(src, buf)]

    @property
    def ref(self):
        for copy in self.copies:
            copy.wait()
        self.copies = []
        return self.buf


SPECS = {"S": SM, "A": pl.BlockSpec(memory_space=pltpu.HBM), "V": pl.BlockSpec(memory_space=pltpu.VMEM)}


def run(body, ins, outs, bufs=(), sems=64, flops=5 * 10**10, name=None, room=6, alias=None):
    n_in, n_out = len(ins), len(outs)

    def kernel(*refs):
        copies = Copies(refs[-1])
        body(copies, refs[:n_in], refs[n_in : n_in + n_out], refs[n_in + n_out : -1])
        copies.finish()

    scratch = sum(math.prod(shape) * jnp.dtype(d).itemsize for shape, d in bufs)
    return pl.pallas_call(
        kernel,
        out_shape=[jax.ShapeDtypeStruct(o[0], o[1]) for o in outs],
        in_specs=[SPECS[k] for _, k in ins],
        out_specs=[SPECS[o[2]] for o in outs],
        scratch_shapes=[pltpu.VMEM(shape, d) for shape, d in bufs] + [pltpu.SemaphoreType.DMA((sems,))],
        compiler_params=pltpu.CompilerParams(vmem_limit_bytes=scratch + room * 2**20),
        cost_estimate=pl.CostEstimate(flops=flops, bytes_accessed=1, transcendentals=0),
        name=name,
        input_output_aliases=alias or {},
    )(*ins_only(ins))


def ins_only(ins):
    return [a for a, _ in ins]


def kind(k, *arrays):
    return [(a, k) for a in arrays]


def step_bits(n):
    bits = [1 << p for p in range(1, n.bit_length() - 1)]
    return bits[::-1], bits


def masks(bits):
    k = len(bits)
    found = []
    for s in range(1 << k):
        m = 0
        for p in range(k):
            if not (s >> (k - 1 - p)) & 1:
                m ^= bits[p]
        found.append(m)
    return found


def swap_core(x, n):
    return lax.ppermute(x, "fsdp", [(i, i ^ 1) for i in range(n)])


def swap_step(x, n, p, flip=False):
    even, odd = step_bits(n)[::-1] if flip else step_bits(n)
    return lax.ppermute(x, "fsdp", [(i, i ^ (odd[p] if i & 1 else even[p])) for i in range(n)])


def after(x, *others):
    return lax.optimization_barrier((x,) + others)[0]


def gather_masks(n):
    return list(range(0, n, 2)) + list(range(1, n, 2))


class Gather:
    def __init__(self, x, n):
        self.n = n
        self.have = [x] + [lax.ppermute(x, "fsdp", [(i, i ^ m) for i in range(n)]) for m in range(2, n, 2)]

    def pieces(self, *others):
        return self.have + [swap_core(after(t, *others), self.n) for t in self.have]


def add_parts(parts, rows, last=False):
    total = sum(a[f : f + rows].astype(F32) for a, f in parts)
    return total if last else lax.optimization_barrier(total.astype(BF))


def swap_dp(x, n, d, even, odd):
    pairs = []
    for z in range(d):
        for i in range(n):
            pairs.append((z * n + i, (z ^ (odd if i & 1 else even)) * n + i))
    return lax.ppermute(x, ("dp", "fsdp"), pairs)


def dp_steps(d):
    bits = [1 << p for p in range(d.bit_length() - 1)]
    return list(zip(bits, bits[::-1]))


class Sum:
    def __init__(self, n, d, send, keeps, flip=False):
        self.n, self.d, self.keeps, self.step, self.flip = n, d, keeps, 0, flip
        self.got = [(swap_core(send, n), 0)]
        self.own = None
        self.dp = dp_steps(d) if d & (d - 1) == 0 else None

    def advance(self, *others, send=True):
        if self.step < len(self.keeps):
            keep = self.keeps[self.step]
            rows = keep.shape[0]
            mine = add_parts([(after(keep, *others), 0)] + self.got, rows)
            self.got = [(a, f + rows) for a, f in self.got]
            if self.step < len(self.keeps) - 1:
                self.got.append((swap_step(mine, self.n, self.step, self.flip), 0))
            else:
                self.own = mine
                self.send_dp()
        else:
            rows = self.own.shape[0]
            end = self.step == len(self.keeps) + len(self.dp) - 1
            mine = self.own = add_parts([(after(self.own, *others), 0), (self.arrive, 0)], rows, end)
            if send:
                self.send_dp()
        self.step += 1
        return mine

    def send_later(self, *others):
        self.step -= 1
        self.send_dp(*others)
        self.step += 1

    def send_dp(self, *others):
        at = self.step - len(self.keeps) + 1
        if self.dp is None:
            self.own = lax.psum(self.own, "dp")
        elif at < len(self.dp):
            self.arrive = swap_dp(after(self.own, *others), self.n, self.d, *self.dp[at])

    def end(self):
        last = len(self.keeps) + (0 if self.dp is None else len(self.dp))
        while self.step < last:
            self.advance()
        return self.own


def staggered(keys, product, use):
    ahead = product(*keys[0])
    for i, key in enumerate(keys):
        now = ahead
        if i + 1 < len(keys):
            ahead = product(*keys[i + 1])
        use(*key, now)


def norm_stats(x):
    mu = jnp.mean(x, -1, keepdims=True)
    c = x - mu
    rs = lax.rsqrt(jnp.mean(c * c, -1, keepdims=True) + EPS)
    return c * rs, rs


def softmax_rows(s):
    m = jnp.max(s, 0, keepdims=True)
    e = jnp.exp2(s - m)
    return e.astype(BF), 1.0 / jnp.sum(e, 0, keepdims=True)


def same_block(seg_ref, b):
    row = jnp.broadcast_to(seg_ref[:, b * DB : (b + 1) * DB].astype(F32), (DB, DB))
    return row == row.T


def piece_block(n, r):
    return lax.axis_index("fsdp") ^ gather_masks(n)[r]


def slot_block(n, s, flip=False):
    me = lax.axis_index("fsdp")
    even, odd = (masks(b) for b in (step_bits(n)[::-1] if flip else step_bits(n)))
    if s < n // 2:
        return me ^ jnp.where((me & 1) == 1, odd[s], even[s])
    s -= n // 2
    return me ^ 1 ^ jnp.where((me & 1) == 1, even[s], odd[s])


def is_big(seg_ref):
    last = seg_ref[:, HALF - 128 : HALF].astype(F32)
    lane = lax.broadcasted_iota(jnp.int32, (1, 128), 1)
    return jnp.max(jnp.where(lane == 127, last, -1.0)) == 0.0


def place(copies, n, pieces, first, rows, buf, col=0):
    started = []
    for r in range(n):
        here = pl.ds(pl.multiple_of(piece_block(n, r) * rows, rows), rows)
        started.append(copies.start(pieces[r].at[pl.ds(first, rows), :], buf.at[here, pl.ds(col, D)]))
    return started


def wait_all(started):
    for copy in started:
        copy.wait()


def pack_body(n, copies, ins, outs, bufs):
    wq, wo, wu = ins[:3]
    vecs = ins[3:]
    a_o, b_o = outs
    rows = wq.shape[0]
    a, b = bufs[:2]
    vbufs = bufs[2:]
    mats = [copies.start(wq.at[:, pl.ds(c * D, D)], a.at[pl.ds(c * rows, rows), :]) for c in range(3)]
    held = [Held(copies, v, vb) for v, vb in zip(vecs, vbufs)]
    rest = [copies.start(wo, b.at[pl.ds(0, rows), :])]
    for c in range(4):
        rest.append(copies.start(wu.at[:, pl.ds(c * D, D)], b.at[pl.ds((1 + c) * rows, rows), :]))
    full = []
    for h in held:
        g = h.ref[...].astype(F32).reshape(1, -1)
        full.append(jnp.concatenate([g] * (D // g.shape[1]), 1))
    full.append(jnp.zeros((BIAS - len(full), D), F32))
    a[pl.ds(3 * rows, BIAS), :] = jnp.concatenate(full, 0).astype(BF)
    wait_all(mats)
    copies.send(a, a_o)
    wait_all(rest)
    copies.send(b, b_o)


def qkv_body(n, rows, copies, ins, outs, bufs):
    x_h = ins[0]
    pieces = ins[1:]
    bias_b, w, h1_b, q, k, v, kt, vt = outs
    x, lines = bufs
    t = x.shape[0]
    x = Held(copies, x_h, x)
    vecs = [copies.start(pieces[r].at[pl.ds(3 * rows, BIAS), :], lines.at[r]) for r in range(n)]
    parts = [place(copies, n, pieces, c * rows, rows, w, c * D) for c in range(3)]
    wait_all(vecs)
    lane = lax.broadcasted_iota(jnp.int32, (BIAS, D), 1)
    bias = jnp.zeros((BIAS, D), F32)
    ub = [jnp.zeros((1, D), F32) for _ in range(4)]
    for r in range(n):
        j = piece_block(n, r)
        got = lines[r].astype(F32)
        bias = jnp.where(lane // (D // n) == j, got, bias)
        for c in range(4):
            ub[c] = jnp.where(c * (n // 4) + lane[:1, :] // (FF // n) == j, got[UB : UB + 1, :], ub[c])
    bias_b[0:BIAS, :] = bias
    for c in range(4):
        bias_b[UB + c : UB + c + 1, :] = ub[c]
    xr = x.ref
    tile = 256
    for started in parts:
        wait_all(started)

    def norm(at):
        nrm, _ = norm_stats(xr[at, :].astype(F32))
        h1 = (nrm * bias[G1 : G1 + 1, :] + bias[C1 : C1 + 1, :]).astype(BF)
        h1_b[at, :] = h1
        return h1

    def project(at, h1):
        q[at, :] = ((mm(h1, w[:, :D], NN) + bias[QB : QB + 1, :]) * QSCALE).astype(BF)
        kk = mm(h1, w[:, D : 2 * D], NN).astype(BF)
        k[at, :] = kk
        kt[:, at] = kk.T
        vv = (mm(h1, w[:, 2 * D :], NN) + bias[VB : VB + 1, :]).astype(BF)
        v[at, :] = vv
        vt[:, at] = vv.T

    staggered([(slice(i * tile, (i + 1) * tile),) for i in range(t // tile)], norm, project)


def attn_body(n, copies, ins, outs, bufs):
    seg, q, k, vt = ins
    ot, linv_b, e_b, ed_b = outs
    t = q.shape[0]
    nh = HALF // DB
    big = is_big(seg)

    def head(h):
        return slice(h * HD, (h + 1) * HD)

    def finish(h, at, e, linv):
        ot[head(h), at] = (mm(vt[head(h), at], e, NN) * linv).astype(BF)
        linv_b[h : h + 1, at] = linv

    def dense():
        at = slice(0, HALF)
        ahead = mm(k[at, head(0)], q[at, head(0)], NT)
        for h in range(HEADS):
            s = ahead
            if h + 1 < HEADS:
                ahead = mm(k[at, head(h + 1)], q[at, head(h + 1)], NT)
            e, linv = softmax_rows(s)
            e_b[h] = e
            finish(h, at, e, linv)

    def diagonal(blocks):
        keys = [(b, h) for b in blocks for h in range(HEADS)]
        at = {b: slice(b * DB, (b + 1) * DB) for b in blocks}
        same = {b: same_block(seg, b) for b in blocks}
        s = [mm(k[at[b], head(h)], q[at[b], head(h)], NT) for b, h in keys]
        r = [softmax_rows(jnp.where(same[b], x, MASKED)) for (b, h), x in zip(keys, s)]
        for (b, h), (e, _) in zip(keys, r):
            if b < nh:
                e_b[h, at[b], :DB] = e
            else:
                ed_b[h, b - nh] = e
        for (b, h), (e, linv) in zip(keys, r):
            finish(h, at[b], e, linv)

    pl.when(big)(dense)

    @pl.when(jnp.logical_not(big))
    def _():
        for b in range(0, nh, 2):
            diagonal((b, b + 1))

    for b in range(nh, t // DB, 2):
        diagonal((b, b + 1))


def send_slots(copies, n, outs, rows, put, flip=False):
    send_h, keeps = outs[0], outs[1:]
    s = 0
    for ref in list(keeps) + [send_h]:
        for i in range(ref.shape[0] // rows):
            put(slot_block(n, s, flip), s, ref, i * rows)
            s += 1


def mlp_up_body(n, rows, copies, ins, outs, bufs):
    x_h, ot, bias = ins[:3]
    pieces = ins[3:]
    wo, wu, x2, h2, z, gd = outs
    (x,) = bufs
    t = x.shape[0]
    fr = FF // n
    started = place(copies, n, pieces, 0, rows, wo)
    x = Held(copies, x_h, x)
    ups = [place(copies, n, pieces, (1 + c) * rows, rows, wu, c * D) for c in range(4)]
    wait_all(started)
    x = x.ref
    tile = 256
    rows_at = [slice(i * tile, (i + 1) * tile) for i in range(t // tile)]
    gain, shift = bias[G2 : G2 + 1, :], bias[C2 : C2 + 1, :]

    def branch(at):
        return mm(ot[:, at], wo[...], TN)

    def norm(at, got):
        v = x[at, :].astype(F32) + got + bias[OB : OB + 1, :]
        x2[at, :] = v
        nrm, _ = norm_stats(v)
        h2[at, :] = (nrm * gain + shift).astype(BF)

    staggered([(at,) for at in rows_at], branch, norm)
    for c in range(4):
        wait_all(ups[c])

    def hidden(at, c):
        return mm(h2[at, :], wu[:, c * D : (c + 1) * D], NN)

    def act(at, c, got):
        cs = slice(c * D, (c + 1) * D)
        v = got + bias[UB + c : UB + c + 1, :]
        v2 = v * v
        hh = 0.5 * jnp.tanh(v * (CK + (CK * CA) * v2)) + 0.5
        zz = v * hh
        z[at, cs] = zz.astype(BF)
        gd[at, cs] = (hh + zz * (1.0 - hh) * (2.0 * CK + (6.0 * CK * CA) * v2)).astype(BF)

    staggered([(at, c) for at in rows_at for c in range(4)], hidden, act)


def mlp_down_body(n, copies, ins, outs, bufs):
    z, x2, gm_h = ins
    gm, acc = bufs
    gm = Held(copies, gm_h, gm)
    copies.send(z, outs[0])
    copies.send(x2, outs[1])
    gm = gm.ref
    fr = FF // n
    per = D // fr
    for c in range(4):
        acc[pl.ds(c * per, per)] = mm(z[:, c * D : (c + 1) * D], gm[...], TN).astype(BF).reshape(per, fr, D)

    def put(j, s, dst, lo):
        dst[lo : lo + fr, :] = acc[j]

    send_slots(copies, n, outs[2:], fr, put)


def mlp_back_body(n, copies, ins, outs, bufs):
    gm_h, gd = ins[:2]
    pieces = ins[2:]
    wd_h, gu, sums = outs
    gm, wd = bufs
    t = gm.shape[0]
    gm = Held(copies, gm_h, gm)
    wds = place(copies, n, pieces, 0, FF // n, wd)
    gm = gm.ref
    wait_all(wds)
    copies.send(wd, wd_h)
    tile = 256
    ubs = [jnp.zeros((1, D), F32) for _ in range(4)]
    dbs = jnp.zeros((1, D), F32)
    rows_at = [slice(i * tile, (i + 1) * tile) for i in range(t // tile)]

    def product(at, c):
        return mm(gm[at, :], wd[c * D : (c + 1) * D, :], NT)

    def use(at, c, got):
        cs = slice(c * D, (c + 1) * D)
        part = (got * gd[at, cs].astype(F32)).astype(BF)
        gu[at, cs] = part
        ubs[c] += jnp.sum(part.astype(F32), 0, keepdims=True)

    staggered([(at, c) for at in rows_at for c in range(4)], product, use)
    for at in rows_at:
        dbs += jnp.sum(gm[at, :].astype(F32), 0, keepdims=True)
    sums[...] = jnp.zeros_like(sums)
    sums[DBI : DBI + 1, :] = dbs
    for c in range(4):
        sums[UB + c : UB + c + 1, :] = ubs[c]


def norm_back_body(copies, ins, outs, bufs):
    gu, wu, x2, bias, wo, linv, ot, sums, gm_h = ins
    ga, got, drow, bg = outs
    (gm,) = bufs
    t = x2.shape[0]
    gm = Held(copies, gm_h, gm)
    tile = 256
    gain = bias[G2 : G2 + 1, :]
    gm = gm.ref
    rows_at = [slice(i * tile, (i + 1) * tile) for i in range(t // tile)]
    total = [jnp.zeros((1, D), F32) for _ in range(3)]

    def back(at):
        return mm(gu[at, :], wu[...], NT)

    def norm(at, r):
        nrm, rs = norm_stats(x2[at, :])
        rn = r * nrm
        total[0] += jnp.sum(rn, 0, keepdims=True)
        total[1] += jnp.sum(r, 0, keepdims=True)
        dn = r * gain
        dv = rs * (dn - jnp.mean(dn, -1, keepdims=True) - nrm * jnp.mean(rn * gain, -1, keepdims=True))
        out = (gm[at, :].astype(F32) + dv).astype(BF)
        ga[at, :] = out
        total[2] += jnp.sum(out.astype(F32), 0, keepdims=True)

    staggered([(at,) for at in rows_at], back, norm)
    g2s, c2s, obs = total

    def product(at):
        return mm(wo[...], ga[at, :], NT)

    def use(at, got_f):
        for h in range(HEADS):
            hs = slice(h * HD, (h + 1) * HD)
            gs = (got_f[hs, :] * linv[h : h + 1, at]).astype(BF)
            got[hs, at] = gs
            drow[h : h + 1, at] = jnp.sum(gs.astype(F32) * ot[hs, at].astype(F32), 0, keepdims=True)

    staggered([(at,) for at in rows_at], product, use)
    bg[...] = sums[...]
    bg[OB : OB + 1, :] = obs
    bg[G2 : G2 + 1, :] = g2s
    bg[C2 : C2 + 1, :] = c2s


def mlp_grad_body(n, rows, copies, ins, outs, bufs):
    ot, ga, h2, gu = ins
    acc_up, acc_out = bufs
    acc_out[...] = mm(ot[...], ga[...], NN).astype(BF)

    acc_up[...] = mm(h2[...], gu[...], TN).astype(BF)

    def put(j, s, dst, lo):
        here = pl.ds(pl.multiple_of(j * rows, rows), rows)
        dst[lo : lo + rows, :] = acc_out[here, :]
        for c in range(4):
            dst[lo + (1 + c) * rows : lo + (2 + c) * rows, :] = acc_up[here, c * D : (c + 1) * D]

    send_slots(copies, n, outs, 5 * rows, put)


def head(h):
    return slice(h * HD, (h + 1) * HD)


def back_dense(e, v, got, drow, kt, q, gqt, gk, gv):
    at = slice(0, HALF)
    ahead = mm(v[at, head(0)], got[head(0), at], NN)
    for h in range(HEADS):
        hs, dp = head(h), ahead
        if h + 1 < HEADS:
            ahead = mm(v[at, head(h + 1)], got[head(h + 1), at], NN)
        prob = e[h]
        ds = (prob.astype(F32) * (dp - drow[h : h + 1, at])).astype(BF)
        gqt[hs, at] = (mm(kt[hs, at], ds, NN) * 0.125).astype(BF)
        gk[at, hs] = (mm(ds, q[at, hs], NN) * LN2).astype(BF)
        gv[at, hs] = mm(prob, got[hs, at], NT).astype(BF)


def back_blocks(blocks, prob, v, got, drow, kt, q, gqt, gk, gv):
    keys = [(b, h) for b in blocks for h in range(HEADS)]
    at = {b: slice(b * DB, (b + 1) * DB) for b in blocks}
    dp = [mm(v[at[b], head(h)], got[head(h), at[b]], NN) for b, h in keys]
    pv = [mm(prob(b, h), got[head(h), at[b]], NT) for b, h in keys]
    ds = [
        (prob(b, h).astype(F32) * (x - drow[h : h + 1, at[b]])).astype(BF) for (b, h), x in zip(keys, dp)
    ]
    pq = [mm(kt[head(h), at[b]], x, NN) for (b, h), x in zip(keys, ds)]
    pk = [mm(x, q[at[b], head(h)], NN) for (b, h), x in zip(keys, ds)]
    for i, (b, h) in enumerate(keys):
        gqt[head(h), at[b]] = (pq[i] * 0.125).astype(BF)
        gk[at[b], head(h)] = (pk[i] * LN2).astype(BF)
        gv[at[b], head(h)] = pv[i].astype(BF)


def attn_back_body(n, copies, ins, outs, bufs):
    seg, v, got, drow, e, kt, q = ins
    gqt, gk, gv = outs
    big = is_big(seg)

    @pl.when(big)
    def _():
        back_dense(e, v, got, drow, kt, q, gqt, gk, gv)

    @pl.when(jnp.logical_not(big))
    def _():
        def prob(b, h):
            return e[h, b * DB : (b + 1) * DB, :DB]

        for b in range(0, HALF // DB, 2):
            back_blocks((b, b + 1), prob, v, got, drow, kt, q, gqt, gk, gv)


def qkv_back_body(copies, ins, outs, bufs):
    v, got, drow, ed, kt, q, gqt0, gk0, gv0, wq, ga, x_h, bias, bg = ins
    tg_h, g, full_b = outs
    x, gqt, gk, gv, tg = bufs
    x = Held(copies, x_h, x)
    t = x_h.shape[0]
    nb, nh = t // DB, HALF // DB
    for b in range(nh, nb, 2):
        back_blocks((b, b + 1), lambda b, h: ed[h, b - nh], v, got, drow, kt, q, gqt, gk, gv)
    g[:HALF, :D] = gqt0[...].T
    g[HALF:, :D] = gqt[:, HALF:].T
    g[:HALF, D : 2 * D] = gk0[...]
    g[HALF:, D : 2 * D] = gk[HALF:, :]
    g[:HALF, 2 * D :] = gv0[...]
    g[HALF:, 2 * D :] = gv[HALF:, :]

    tile = 256
    x = x.ref
    gain = bias[G1 : G1 + 1, :]
    rows_at = [slice(i * tile, (i + 1) * tile) for i in range(t // tile)]
    total = [jnp.zeros((1, D), F32) for _ in range(4)]

    def back(at):
        return mm(g[at, :], wq[...], NT)

    def norm(at, r):
        nrm, rs = norm_stats(x[at, :].astype(F32))
        rn = r * nrm
        total[0] += jnp.sum(rn, 0, keepdims=True)
        total[1] += jnp.sum(r, 0, keepdims=True)
        total[2] += jnp.sum(g[at, :D].astype(F32), 0, keepdims=True)
        total[3] += jnp.sum(g[at, 2 * D :].astype(F32), 0, keepdims=True)
        dn = r * gain
        dv = rs * (dn - jnp.mean(dn, -1, keepdims=True) - nrm * jnp.mean(rn * gain, -1, keepdims=True))
        tg[at, :] = (ga[at, :].astype(F32) + dv).astype(BF)
        copies.send(tg.at[at, :], tg_h.at[at, :])

    staggered([(at,) for at in rows_at], back, norm)
    g1s, c1s, qbs, vbs = total
    row = lax.broadcasted_iota(jnp.int32, (BIAS, D), 0)
    full = bg[...]
    for at, val in ((QB, qbs), (VB, vbs), (G1, g1s), (C1, c1s)):
        full = jnp.where(row == at, val, full)
    full_b[...] = full.astype(BF)


def qkv_grad_body(n, rows, copies, ins, outs, bufs):
    h1, g, lines = ins
    (acc,) = bufs
    acc[...] = mm(h1[...], g[...], TN).astype(BF)

    def put(j, s, dst, lo):
        here = pl.ds(pl.multiple_of(j * rows, rows), rows)
        for c in range(3):
            dst[lo + c * rows : lo + (1 + c) * rows, :] = acc[here, c * D : (c + 1) * D]
        dst[lo + 3 * rows : lo + 3 * rows + BIAS, :] = lines[...]

    send_slots(copies, n, outs, 3 * rows + BIAS, put, True)


def mixed_body(first, copies, ins, outs, bufs):
    z_h, wd_h, x2_h, bias, live = ins[:5]
    z, wd, x2, mixed = bufs
    t = mixed.shape[0]
    tile = 256
    wd, x2 = Held(copies, wd_h, wd), Held(copies, x2_h.at[pl.ds(first, t), :], x2)
    zs = [
        copies.start(z_h.at[pl.ds(first + i * tile, tile), :], z.at[pl.ds(i * tile, tile), :]) for i in range(t // tile)
    ]
    cols = jnp.broadcast_to(live[:, first : first + t].astype(F32), (128, t)).T
    wd, x2 = wd.ref, x2.ref

    def product(i):
        zs[i].wait()
        return mm(z[i * tile : (i + 1) * tile, :], wd[...], NN)

    def use(i, got):
        at = slice(i * tile, (i + 1) * tile)
        out = x2[at, :] + got + bias[DBI : DBI + 1, :]
        mixed[at, :] = jnp.where(cols[at, :1] >= 0, out, 0.0).astype(BF)
        copies.send(mixed.at[pl.ds(i * tile, tile), :], outs[0].at[pl.ds(first + i * tile, tile), :])

    staggered([(i,) for i in range(t // tile)], product, use)


def on_device(n, d, tokens, segments, cotangent, w_qkv, w_out, w_up, w_down, *vectors):
    t = tokens.shape[0]
    rows = w_qkv.shape[0]
    fr = w_down.shape[0]
    nb, nh = t // DB, HALF // DB
    me = lax.axis_index("fsdp")
    qb, vb, ob, ub, db, g1, c1, g2, c2 = vectors
    lines = [qb, vb, ob, db, g1, c1, g2, c2, ub]
    ra, rb, rc = 3 * rows + BIAS, 5 * rows, fr
    pack_a, pack_b = run(
        functools.partial(pack_body, n),
        kind("A", w_qkv, w_out, w_up, *lines),
        [((ra, D), BF, "A"), ((rb, D), BF, "A")],
        [((ra, D), BF), ((rb, D), BF)] + [(a.shape, BF) for a in lines],
        name="pack",
        room=58,
    )
    a = Gather(pack_a, n)
    b = Gather(pack_b, n)
    got_a = a.pieces()
    c = Gather(after(w_down, a.have[1]), n)
    live = (segments >= 0)[:, None]
    gm = jnp.where(live, cotangent, jnp.zeros_like(cotangent))
    seg_row = segments[None, :]

    tok, tokt, wide = ((t, D), BF), ((D, t), BF), ((t, FF), BF)
    hrow, bias_s, tokf = ((HEADS, t), F32), ((BIAS, D), F32), ((t, D), F32)
    bias, wq, h1, q, k, v, kt, vt = run(
        functools.partial(qkv_body, n, rows),
        kind("A", tokens, *got_a),
        [o + ("V",) for o in (bias_s, ((D, 3 * D), BF), tok, tok, tok, tok, tokt, tokt)],
        [tok, ((n, BIAS, D), BF)],
        sems=96,
        flops=10**9,
        name="qkv",
        room=36,
    )
    ot, linv, e, ed = run(
        functools.partial(attn_body, n),
        kind("V", seg_row, after(q, b.have[1]), k, vt),
        [o + ("V",) for o in (tokt, hrow, ((HEADS, HALF, HALF), BF), ((HEADS, nb - nh, DB, DB), BF))],
        flops=10**9,
        name="attn",
    )
    got_b = b.pieces(ot)

    steps = len(step_bits(n)[0])
    counts = [1 << (steps - 1 - p) for p in range(steps)] + [1]

    def slots(r):
        return [((n // 2 * r, D), BF, "V")] + [((m * r, D), BF, "V") for m in counts]

    wo, wu, x2, h2, z, gd = run(
        functools.partial(mlp_up_body, n, rows),
        kind("A", tokens) + kind("V", ot, bias) + kind("A", *got_b),
        [o + ("V",) for o in (((D, D), BF), ((D, FF), BF), tokf, tok, wide, wide)],
        [tok],
        name="mlp_up",
    )
    got_c = c.pieces(h2)
    z_far, x2_far, *down = run(
        functools.partial(mlp_down_body, n),
        kind("V", z, x2) + kind("A", gm),
        [wide + ("A",), tokf + ("A",)] + slots(rc),
        [tok, ((n, rc, D), BF)],
        name="mlp_down",
    )
    down = Sum(n, d, down[0], down[1:])

    wd, gu, sums = run(
        functools.partial(mlp_back_body, n),
        kind("A", gm) + kind("V", gd) + kind("A", *got_c),
        [((FF, D), BF, "A"), wide + ("V",), bias_s + ("V",)],
        [tok, ((FF, D), BF)],
        name="mlp_back",
    )
    s = down.advance(gu)
    ga, got, drow, bg = run(
        norm_back_body,
        kind("V", after(gu, s), wu, x2, bias, wo, linv, ot, sums) + kind("A", gm),
        [o + ("V",) for o in (tok, tokt, hrow, bias_s)],
        [tok],
        name="norm_back",
    )
    up = run(
        functools.partial(mlp_grad_body, n, rows),
        kind("V", ot, ga, h2, gu),
        slots(rb),
        [((D, FF), BF), ((D, D), BF)],
        name="mlp_grad",
    )
    up_sent = up[0]
    up = Sum(n, d, up[0], up[1:])
    s = down.advance(up_sent)
    half, halft = ((HALF, D), BF), ((D, HALF), BF)
    gqt, gk, gv = run(
        functools.partial(attn_back_body, n),
        kind("V", seg_row, after(v, s), got, drow, e, kt, q),
        [o + ("V",) for o in (halft, half, half)],
        name="attn_back",
    )
    r = up.advance(gk)
    s = down.advance(gk, r)
    tokens_grad, g, lines_b = run(
        qkv_back_body,
        kind("V", after(v, s, r), got, drow, ed, kt, q, gqt, gk, gv, wq, ga) + kind("A", tokens) + kind("V", bias, bg),
        [tok + ("A",), ((t, 3 * D), BF, "V"), ((BIAS, D), BF, "V")],
        [tok, tokt, tok, tok, tok],
        name="qkv_back",
    )
    last = run(
        functools.partial(qkv_grad_body, n, rows),
        kind("V", h1, g, lines_b),
        slots(ra),
        [((D, 3 * D), BF)],
        sems=128,
        name="qkv_grad",
    )
    s = down.advance(last[0], send=False)
    last_sent = after(last[0], s)
    last = Sum(n, d, last_sent, last[1:], True)
    r = up.advance(last_sent)
    down.send_later(r)
    r = last.advance(r)
    def half_mixed(part, hold, *before):
        (out,) = run(
            functools.partial(mixed_body, part * (t // 2)),
            kind("A", after(z_far, hold), wd, x2_far) + kind("V", bias, seg_row) + kind("A", *before),
            [tok + ("A",)],
            [((t // 2, FF), BF), ((FF, D), BF), ((t // 2, D), F32), ((t // 2, D), BF)],
            name="mixed" + str(part),
            alias={5: 0} if before else None,
        )
        return out

    mixed = half_mixed(0, r)
    s = up.advance(mixed)
    r = last.advance(s)
    mixed = half_mixed(1, r, mixed)
    s = down.advance(mixed)
    r = last.advance(s)
    s = up.advance(r)
    r = last.advance(s)
    s = up.advance(r)
    r = last.advance(s)
    down, up, last = down.end(), up.end(), last.end()
    part = D // n
    first = me * part
    vec = lax.dynamic_slice(last, (3 * rows, first), (BIAS, part)).astype(F32)
    ubg = lax.dynamic_slice(last[3 * rows + UB : 3 * rows + UB + 4, :].reshape(-1), (me * fr,), (fr,)).astype(F32)
    qkv_grad = jnp.concatenate([last[c * rows : (c + 1) * rows] for c in range(3)], 1).astype(F32)
    up_grad = jnp.concatenate([up[(1 + c) * rows : (2 + c) * rows] for c in range(4)], 1).astype(F32)
    return (
        mixed,
        tokens_grad,
        qkv_grad,
        up[:rows].astype(F32),
        up_grad,
        down.astype(F32),
        vec[QB],
        vec[VB],
        vec[OB],
        ubg,
        vec[DBI],
        vec[G1],
        vec[C1],
        vec[G2],
        vec[C2],
    )


def solution(mesh):
    rows = P(("dp", "fsdp"), None)
    mat, vec = P("fsdp", None), P("fsdp")
    return jax.shard_map(
        functools.partial(on_device, mesh.shape["fsdp"], mesh.shape["dp"]),
        mesh=mesh,
        in_specs=(rows, P(("dp", "fsdp")), rows) + (mat,) * 4 + (vec,) * 9,
        out_specs=(rows, rows) + (mat,) * 4 + (vec,) * 9,
        check_vma=False,
    )
```

```python
import functools
import math

import jax
import jax.numpy as jnp
from jax import lax
from jax.experimental import pallas as pl
from jax.experimental.pallas import tpu as pltpu
from jax.sharding import PartitionSpec as P

D = 512
HEADS = 8
HD = 64
FF = 2048
HALF = 512
DB = 128
BIAS = 16
EPS = 1e-05
MASKED = -1e30
F32 = jnp.float32
BF = jnp.bfloat16
LOG2E = math.log2(math.e)
QSCALE = 0.125 * LOG2E
LN2 = math.log(2.0)
CK = math.sqrt(2.0 / math.pi)
CA = 0.044715
NN = (((1,), (0,)), ((), ()))
NT = (((1,), (1,)), ((), ()))
TN = (((0,), (0,)), ((), ()))

SM = pl.BlockSpec(memory_space=pltpu.SMEM)
QB, VB, OB, DBI, G1, C1, G2, C2, UB = range(9)


def mm(a, b, dims):
    return lax.dot_general(a, b, dims, preferred_element_type=F32)


class Copies:
    def __init__(self, sems):
        self.sems, self.used, self.out = sems, 0, []

    def start(self, src, dst):
        copy = pltpu.make_async_copy(src, dst, self.sems.at[self.used])
        self.used += 1
        copy.start()
        return copy

    def send(self, src, dst):
        self.out.append(self.start(src, dst))

    def finish(self):
        for copy in self.out:
            copy.wait()


class Held:
    def __init__(self, copies, src, buf):
        self.buf, self.copies = buf, [copies.start(src, buf)]

    @property
    def ref(self):
        for copy in self.copies:
            copy.wait()
        self.copies = []
        return self.buf


SPECS = {"S": SM, "A": pl.BlockSpec(memory_space=pltpu.HBM), "V": pl.BlockSpec(memory_space=pltpu.VMEM)}


def run(body, ins, outs, bufs=(), sems=64, flops=5 * 10**10, name=None, room=6, alias=None):
    n_in, n_out = len(ins), len(outs)

    def kernel(*refs):
        copies = Copies(refs[-1])
        body(copies, refs[:n_in], refs[n_in : n_in + n_out], refs[n_in + n_out : -1])
        copies.finish()

    scratch = sum(math.prod(shape) * jnp.dtype(d).itemsize for shape, d in bufs)
    return pl.pallas_call(
        kernel,
        out_shape=[jax.ShapeDtypeStruct(o[0], o[1]) for o in outs],
        in_specs=[SPECS[k] for _, k in ins],
        out_specs=[SPECS[o[2]] for o in outs],
        scratch_shapes=[pltpu.VMEM(shape, d) for shape, d in bufs] + [pltpu.SemaphoreType.DMA((sems,))],
        compiler_params=pltpu.CompilerParams(vmem_limit_bytes=scratch + room * 2**20),
        cost_estimate=pl.CostEstimate(flops=flops, bytes_accessed=1, transcendentals=0),
        name=name,
        input_output_aliases=alias or {},
    )(*ins_only(ins))


def ins_only(ins):
    return [a for a, _ in ins]


def kind(k, *arrays):
    return [(a, k) for a in arrays]


def step_bits(n):
    bits = [1 << p for p in range(1, n.bit_length() - 1)]
    return bits[::-1], bits


def masks(bits):
    k = len(bits)
    found = []
    for s in range(1 << k):
        m = 0
        for p in range(k):
            if not (s >> (k - 1 - p)) & 1:
                m ^= bits[p]
        found.append(m)
    return found


def swap_core(x, n):
    return lax.ppermute(x, "fsdp", [(i, i ^ 1) for i in range(n)])


def swap_step(x, n, p, flip=False):
    even, odd = step_bits(n)[::-1] if flip else step_bits(n)
    return lax.ppermute(x, "fsdp", [(i, i ^ (odd[p] if i & 1 else even[p])) for i in range(n)])


def after(x, *others):
    return lax.optimization_barrier((x,) + others)[0]


def gather_masks(n):
    return list(range(0, n, 2)) + list(range(1, n, 2))


class Gather:
    def __init__(self, x, n):
        self.n = n
        self.have = [x] + [lax.ppermute(x, "fsdp", [(i, i ^ m) for i in range(n)]) for m in range(2, n, 2)]

    def pieces(self, *others):
        return self.have + [swap_core(after(t, *others), self.n) for t in self.have]


def add_parts(parts, rows, last=False):
    total = sum(a[f : f + rows].astype(F32) for a, f in parts)
    return total if last else lax.optimization_barrier(total.astype(BF))


def swap_dp(x, n, d, even, odd):
    pairs = []
    for z in range(d):
        for i in range(n):
            pairs.append((z * n + i, (z ^ (odd if i & 1 else even)) * n + i))
    return lax.ppermute(x, ("dp", "fsdp"), pairs)


def dp_steps(d):
    bits = [1 << p for p in range(d.bit_length() - 1)]
    return list(zip(bits, bits[::-1]))


class Sum:
    def __init__(self, n, d, send, keeps, flip=False):
        self.n, self.d, self.keeps, self.step, self.flip = n, d, keeps, 0, flip
        self.got = [(swap_core(send, n), 0)]
        self.own = None
        self.dp = dp_steps(d) if d & (d - 1) == 0 else None

    def advance(self, *others, send=True):
        if self.step < len(self.keeps):
            keep = self.keeps[self.step]
            rows = keep.shape[0]
            mine = add_parts([(after(keep, *others), 0)] + self.got, rows)
            self.got = [(a, f + rows) for a, f in self.got]
            if self.step < len(self.keeps) - 1:
                self.got.append((swap_step(mine, self.n, self.step, self.flip), 0))
            else:
                self.own = mine
                self.send_dp()
        else:
            rows = self.own.shape[0]
            end = self.step == len(self.keeps) + len(self.dp) - 1
            mine = self.own = add_parts([(after(self.own, *others), 0), (self.arrive, 0)], rows, end)
            if send:
                self.send_dp()
        self.step += 1
        return mine

    def send_later(self, *others):
        self.step -= 1
        self.send_dp(*others)
        self.step += 1

    def send_dp(self, *others):
        at = self.step - len(self.keeps) + 1
        if self.dp is None:
            self.own = lax.psum(self.own, "dp")
        elif at < len(self.dp):
            self.arrive = swap_dp(after(self.own, *others), self.n, self.d, *self.dp[at])

    def end(self):
        last = len(self.keeps) + (0 if self.dp is None else len(self.dp))
        while self.step < last:
            self.advance()
        return self.own


def staggered(keys, product, use):
    ahead = product(*keys[0])
    for i, key in enumerate(keys):
        now = ahead
        if i + 1 < len(keys):
            ahead = product(*keys[i + 1])
        use(*key, now)


def norm_stats(x):
    mu = jnp.mean(x, -1, keepdims=True)
    c = x - mu
    rs = lax.rsqrt(jnp.mean(c * c, -1, keepdims=True) + EPS)
    return c * rs, rs


def softmax_rows(s):
    m = jnp.max(s, 0, keepdims=True)
    e = jnp.exp2(s - m)
    return e.astype(BF), 1.0 / jnp.sum(e, 0, keepdims=True)


def same_block(seg_ref, b):
    row = jnp.broadcast_to(seg_ref[:, b * DB : (b + 1) * DB].astype(F32), (DB, DB))
    return row == row.T


def piece_block(n, r):
    return lax.axis_index("fsdp") ^ gather_masks(n)[r]


def slot_block(n, s, flip=False):
    me = lax.axis_index("fsdp")
    even, odd = (masks(b) for b in (step_bits(n)[::-1] if flip else step_bits(n)))
    if s < n // 2:
        return me ^ jnp.where((me & 1) == 1, odd[s], even[s])
    s -= n // 2
    return me ^ 1 ^ jnp.where((me & 1) == 1, even[s], odd[s])


def is_big(seg_ref):
    last = seg_ref[:, HALF - 128 : HALF].astype(F32)
    lane = lax.broadcasted_iota(jnp.int32, (1, 128), 1)
    return jnp.max(jnp.where(lane == 127, last, -1.0)) == 0.0


def place(copies, n, pieces, first, rows, buf, col=0):
    started = []
    for r in range(n):
        here = pl.ds(pl.multiple_of(piece_block(n, r) * rows, rows), rows)
        started.append(copies.start(pieces[r].at[pl.ds(first, rows), :], buf.at[here, pl.ds(col, D)]))
    return started


def wait_all(started):
    for copy in started:
        copy.wait()


def pack_body(n, copies, ins, outs, bufs):
    wq, wo, wu = ins[:3]
    vecs = ins[3:]
    a_o, b_o = outs
    rows = wq.shape[0]
    a, b = bufs[:2]
    vbufs = bufs[2:]
    mats = [copies.start(wq.at[:, pl.ds(c * D, D)], a.at[pl.ds(c * rows, rows), :]) for c in range(3)]
    held = [Held(copies, v, vb) for v, vb in zip(vecs, vbufs)]
    rest = [copies.start(wo, b.at[pl.ds(0, rows), :])]
    for c in range(4):
        rest.append(copies.start(wu.at[:, pl.ds(c * D, D)], b.at[pl.ds((1 + c) * rows, rows), :]))
    full = []
    for h in held:
        g = h.ref[...].astype(F32).reshape(1, -1)
        full.append(jnp.concatenate([g] * (D // g.shape[1]), 1))
    full.append(jnp.zeros((BIAS - len(full), D), F32))
    a[pl.ds(3 * rows, BIAS), :] = jnp.concatenate(full, 0).astype(BF)
    wait_all(mats)
    copies.send(a, a_o)
    wait_all(rest)
    copies.send(b, b_o)


def qkv_body(n, rows, copies, ins, outs, bufs):
    x_h = ins[0]
    pieces = ins[1:]
    bias_b, w, h1_b, q, k, v, kt, vt = outs
    x, lines = bufs
    t = x.shape[0]
    x = Held(copies, x_h, x)
    vecs = [copies.start(pieces[r].at[pl.ds(3 * rows, BIAS), :], lines.at[r]) for r in range(n)]
    parts = [place(copies, n, pieces, c * rows, rows, w, c * D) for c in range(3)]
    wait_all(vecs)
    lane = lax.broadcasted_iota(jnp.int32, (BIAS, D), 1)
    bias = jnp.zeros((BIAS, D), F32)
    ub = [jnp.zeros((1, D), F32) for _ in range(4)]
    for r in range(n):
        j = piece_block(n, r)
        got = lines[r].astype(F32)
        bias = jnp.where(lane // (D // n) == j, got, bias)
        for c in range(4):
            ub[c] = jnp.where(c * (n // 4) + lane[:1, :] // (FF // n) == j, got[UB : UB + 1, :], ub[c])
    bias_b[0:BIAS, :] = bias
    for c in range(4):
        bias_b[UB + c : UB + c + 1, :] = ub[c]
    xr = x.ref
    tile = 256
    for started in parts:
        wait_all(started)

    def norm(at):
        nrm, _ = norm_stats(xr[at, :].astype(F32))
        h1 = (nrm * bias[G1 : G1 + 1, :] + bias[C1 : C1 + 1, :]).astype(BF)
        h1_b[at, :] = h1
        return h1

    def project(at, h1):
        q[at, :] = ((mm(h1, w[:, :D], NN) + bias[QB : QB + 1, :]) * QSCALE).astype(BF)
        kk = mm(h1, w[:, D : 2 * D], NN).astype(BF)
        k[at, :] = kk
        kt[:, at] = kk.T
        vv = (mm(h1, w[:, 2 * D :], NN) + bias[VB : VB + 1, :]).astype(BF)
        v[at, :] = vv
        vt[:, at] = vv.T

    staggered([(slice(i * tile, (i + 1) * tile),) for i in range(t // tile)], norm, project)


def attn_body(n, copies, ins, outs, bufs):
    seg, q, k, vt = ins
    ot, linv_b, e_b, ed_b = outs
    t = q.shape[0]
    nh = HALF // DB
    big = is_big(seg)

    def head(h):
        return slice(h * HD, (h + 1) * HD)

    def finish(h, at, e, linv):
        ot[head(h), at] = (mm(vt[head(h), at], e, NN) * linv).astype(BF)
        linv_b[h : h + 1, at] = linv

    def dense():
        at = slice(0, HALF)
        ahead = mm(k[at, head(0)], q[at, head(0)], NT)
        for h in range(HEADS):
            s = ahead
            if h + 1 < HEADS:
                ahead = mm(k[at, head(h + 1)], q[at, head(h + 1)], NT)
            e, linv = softmax_rows(s)
            e_b[h] = e
            finish(h, at, e, linv)

    def diagonal(blocks):
        keys = [(b, h) for b in blocks for h in range(HEADS)]
        at = {b: slice(b * DB, (b + 1) * DB) for b in blocks}
        same = {b: same_block(seg, b) for b in blocks}
        s = [mm(k[at[b], head(h)], q[at[b], head(h)], NT) for b, h in keys]
        r = [softmax_rows(jnp.where(same[b], x, MASKED)) for (b, h), x in zip(keys, s)]
        for (b, h), (e, _) in zip(keys, r):
            if b < nh:
                e_b[h, at[b], :DB] = e
            else:
                ed_b[h, b - nh] = e
        for (b, h), (e, linv) in zip(keys, r):
            finish(h, at[b], e, linv)

    pl.when(big)(dense)

    @pl.when(jnp.logical_not(big))
    def _():
        for b in range(0, nh, 2):
            diagonal((b, b + 1))

    for b in range(nh, t // DB, 2):
        diagonal((b, b + 1))


def send_slots(copies, n, outs, rows, put, flip=False):
    send_h, keeps = outs[0], outs[1:]
    s = 0
    for ref in list(keeps) + [send_h]:
        for i in range(ref.shape[0] // rows):
            put(slot_block(n, s, flip), s, ref, i * rows)
            s += 1


def mlp_up_body(n, rows, copies, ins, outs, bufs):
    x_h, ot, bias = ins[:3]
    pieces = ins[3:]
    wo, wu, x2, h2, z, gd = outs
    (x,) = bufs
    t = x.shape[0]
    fr = FF // n
    started = place(copies, n, pieces, 0, rows, wo)
    x = Held(copies, x_h, x)
    ups = [place(copies, n, pieces, (1 + c) * rows, rows, wu, c * D) for c in range(4)]
    wait_all(started)
    x = x.ref
    tile = 256
    rows_at = [slice(i * tile, (i + 1) * tile) for i in range(t // tile)]
    gain, shift = bias[G2 : G2 + 1, :], bias[C2 : C2 + 1, :]

    def branch(at):
        return mm(ot[:, at], wo[...], TN)

    def norm(at, got):
        v = x[at, :].astype(F32) + got + bias[OB : OB + 1, :]
        x2[at, :] = v
        nrm, _ = norm_stats(v)
        h2[at, :] = (nrm * gain + shift).astype(BF)

    staggered([(at,) for at in rows_at], branch, norm)
    for c in range(4):
        wait_all(ups[c])

    def hidden(at, c):
        return mm(h2[at, :], wu[:, c * D : (c + 1) * D], NN)

    def act(at, c, got):
        cs = slice(c * D, (c + 1) * D)
        v = got + bias[UB + c : UB + c + 1, :]
        v2 = v * v
        hh = 0.5 * jnp.tanh(v * (CK + (CK * CA) * v2)) + 0.5
        zz = v * hh
        z[at, cs] = zz.astype(BF)
        gd[at, cs] = (hh + zz * (1.0 - hh) * (2.0 * CK + (6.0 * CK * CA) * v2)).astype(BF)

    staggered([(at, c) for at in rows_at for c in range(4)], hidden, act)


def mlp_down_body(n, copies, ins, outs, bufs):
    z, x2, gm_h = ins
    gm, acc = bufs
    gm = Held(copies, gm_h, gm)
    copies.send(z, outs[0])
    copies.send(x2, outs[1])
    gm = gm.ref
    fr = FF // n
    per = D // fr
    for c in range(4):
        acc[pl.ds(c * per, per)] = mm(z[:, c * D : (c + 1) * D], gm[...], TN).astype(BF).reshape(per, fr, D)

    def put(j, s, dst, lo):
        dst[lo : lo + fr, :] = acc[j]

    send_slots(copies, n, outs[2:], fr, put)


def mlp_back_body(n, copies, ins, outs, bufs):
    gm_h, gd = ins[:2]
    pieces = ins[2:]
    wd_h, gu, sums = outs
    gm, wd = bufs
    t = gm.shape[0]
    gm = Held(copies, gm_h, gm)
    wds = place(copies, n, pieces, 0, FF // n, wd)
    gm = gm.ref
    wait_all(wds)
    copies.send(wd, wd_h)
    tile = 256
    ubs = [jnp.zeros((1, D), F32) for _ in range(4)]
    dbs = jnp.zeros((1, D), F32)
    rows_at = [slice(i * tile, (i + 1) * tile) for i in range(t // tile)]

    def product(at, c):
        return mm(gm[at, :], wd[c * D : (c + 1) * D, :], NT)

    def use(at, c, got):
        cs = slice(c * D, (c + 1) * D)
        part = (got * gd[at, cs].astype(F32)).astype(BF)
        gu[at, cs] = part
        ubs[c] += jnp.sum(part.astype(F32), 0, keepdims=True)

    staggered([(at, c) for at in rows_at for c in range(4)], product, use)
    for at in rows_at:
        dbs += jnp.sum(gm[at, :].astype(F32), 0, keepdims=True)
    sums[...] = jnp.zeros_like(sums)
    sums[DBI : DBI + 1, :] = dbs
    for c in range(4):
        sums[UB + c : UB + c + 1, :] = ubs[c]


def norm_back_body(copies, ins, outs, bufs):
    gu, wu, x2, bias, wo, linv, ot, sums, gm_h = ins
    ga, got, drow, bg = outs
    (gm,) = bufs
    t = x2.shape[0]
    gm = Held(copies, gm_h, gm)
    tile = 256
    gain = bias[G2 : G2 + 1, :]
    gm = gm.ref
    rows_at = [slice(i * tile, (i + 1) * tile) for i in range(t // tile)]
    total = [jnp.zeros((1, D), F32) for _ in range(3)]

    def back(at):
        return mm(gu[at, :], wu[...], NT)

    def norm(at, r):
        nrm, rs = norm_stats(x2[at, :])
        rn = r * nrm
        total[0] += jnp.sum(rn, 0, keepdims=True)
        total[1] += jnp.sum(r, 0, keepdims=True)
        dn = r * gain
        dv = rs * (dn - jnp.mean(dn, -1, keepdims=True) - nrm * jnp.mean(rn * gain, -1, keepdims=True))
        out = (gm[at, :].astype(F32) + dv).astype(BF)
        ga[at, :] = out
        total[2] += jnp.sum(out.astype(F32), 0, keepdims=True)

    staggered([(at,) for at in rows_at], back, norm)
    g2s, c2s, obs = total

    def product(at):
        return mm(wo[...], ga[at, :], NT)

    def use(at, got_f):
        for h in range(HEADS):
            hs = slice(h * HD, (h + 1) * HD)
            gs = (got_f[hs, :] * linv[h : h + 1, at]).astype(BF)
            got[hs, at] = gs
            drow[h : h + 1, at] = jnp.sum(gs.astype(F32) * ot[hs, at].astype(F32), 0, keepdims=True)

    staggered([(at,) for at in rows_at], product, use)
    bg[...] = sums[...]
    bg[OB : OB + 1, :] = obs
    bg[G2 : G2 + 1, :] = g2s
    bg[C2 : C2 + 1, :] = c2s


def mlp_grad_body(n, rows, copies, ins, outs, bufs):
    ot, ga, h2, gu = ins
    acc_up, acc_out = bufs
    acc_out[...] = mm(ot[...], ga[...], NN).astype(BF)

    acc_up[...] = mm(h2[...], gu[...], TN).astype(BF)

    def put(j, s, dst, lo):
        here = pl.ds(pl.multiple_of(j * rows, rows), rows)
        dst[lo : lo + rows, :] = acc_out[here, :]
        for c in range(4):
            dst[lo + (1 + c) * rows : lo + (2 + c) * rows, :] = acc_up[here, c * D : (c + 1) * D]

    send_slots(copies, n, outs, 5 * rows, put)


def head(h):
    return slice(h * HD, (h + 1) * HD)


def back_dense(e, v, got, drow, kt, q, gqt, gk, gv):
    at = slice(0, HALF)
    ahead = mm(v[at, head(0)], got[head(0), at], NN)
    for h in range(HEADS):
        hs, dp = head(h), ahead
        if h + 1 < HEADS:
            ahead = mm(v[at, head(h + 1)], got[head(h + 1), at], NN)
        prob = e[h]
        ds = (prob.astype(F32) * (dp - drow[h : h + 1, at])).astype(BF)
        gqt[hs, at] = (mm(kt[hs, at], ds, NN) * 0.125).astype(BF)
        gk[at, hs] = (mm(ds, q[at, hs], NN) * LN2).astype(BF)
        gv[at, hs] = mm(prob, got[hs, at], NT).astype(BF)


def back_blocks(blocks, prob, v, got, drow, kt, q, gqt, gk, gv):
    keys = [(b, h) for b in blocks for h in range(HEADS)]
    at = {b: slice(b * DB, (b + 1) * DB) for b in blocks}
    dp = [mm(v[at[b], head(h)], got[head(h), at[b]], NN) for b, h in keys]
    pv = [mm(prob(b, h), got[head(h), at[b]], NT) for b, h in keys]
    ds = [
        (prob(b, h).astype(F32) * (x - drow[h : h + 1, at[b]])).astype(BF) for (b, h), x in zip(keys, dp)
    ]
    pq = [mm(kt[head(h), at[b]], x, NN) for (b, h), x in zip(keys, ds)]
    pk = [mm(x, q[at[b], head(h)], NN) for (b, h), x in zip(keys, ds)]
    for i, (b, h) in enumerate(keys):
        gqt[head(h), at[b]] = (pq[i] * 0.125).astype(BF)
        gk[at[b], head(h)] = (pk[i] * LN2).astype(BF)
        gv[at[b], head(h)] = pv[i].astype(BF)


def attn_back_body(n, copies, ins, outs, bufs):
    seg, v, got, drow, e, kt, q = ins
    gqt, gk, gv = outs
    big = is_big(seg)

    @pl.when(big)
    def _():
        back_dense(e, v, got, drow, kt, q, gqt, gk, gv)

    @pl.when(jnp.logical_not(big))
    def _():
        def prob(b, h):
            return e[h, b * DB : (b + 1) * DB, :DB]

        for b in range(0, HALF // DB, 2):
            back_blocks((b, b + 1), prob, v, got, drow, kt, q, gqt, gk, gv)


def qkv_back_body(copies, ins, outs, bufs):
    v, got, drow, ed, kt, q, gqt0, gk0, gv0, wq, ga, x_h, bias, bg = ins
    tg_h, g, full_b = outs
    x, gqt, gk, gv, tg = bufs
    x = Held(copies, x_h, x)
    t = x_h.shape[0]
    nb, nh = t // DB, HALF // DB
    for b in range(nh, nb, 2):
        back_blocks((b, b + 1), lambda b, h: ed[h, b - nh], v, got, drow, kt, q, gqt, gk, gv)
    g[:HALF, :D] = gqt0[...].T
    g[HALF:, :D] = gqt[:, HALF:].T
    g[:HALF, D : 2 * D] = gk0[...]
    g[HALF:, D : 2 * D] = gk[HALF:, :]
    g[:HALF, 2 * D :] = gv0[...]
    g[HALF:, 2 * D :] = gv[HALF:, :]

    tile = 256
    x = x.ref
    gain = bias[G1 : G1 + 1, :]
    rows_at = [slice(i * tile, (i + 1) * tile) for i in range(t // tile)]
    total = [jnp.zeros((1, D), F32) for _ in range(4)]

    def back(at):
        return mm(g[at, :], wq[...], NT)

    def norm(at, r):
        nrm, rs = norm_stats(x[at, :].astype(F32))
        rn = r * nrm
        total[0] += jnp.sum(rn, 0, keepdims=True)
        total[1] += jnp.sum(r, 0, keepdims=True)
        total[2] += jnp.sum(g[at, :D].astype(F32), 0, keepdims=True)
        total[3] += jnp.sum(g[at, 2 * D :].astype(F32), 0, keepdims=True)
        dn = r * gain
        dv = rs * (dn - jnp.mean(dn, -1, keepdims=True) - nrm * jnp.mean(rn * gain, -1, keepdims=True))
        tg[at, :] = (ga[at, :].astype(F32) + dv).astype(BF)
        copies.send(tg.at[at, :], tg_h.at[at, :])

    staggered([(at,) for at in rows_at], back, norm)
    g1s, c1s, qbs, vbs = total
    row = lax.broadcasted_iota(jnp.int32, (BIAS, D), 0)
    full = bg[...]
    for at, val in ((QB, qbs), (VB, vbs), (G1, g1s), (C1, c1s)):
        full = jnp.where(row == at, val, full)
    full_b[...] = full.astype(BF)


def qkv_grad_body(n, rows, copies, ins, outs, bufs):
    h1, g, lines = ins
    (acc,) = bufs
    acc[...] = mm(h1[...], g[...], TN).astype(BF)

    def put(j, s, dst, lo):
        here = pl.ds(pl.multiple_of(j * rows, rows), rows)
        for c in range(3):
            dst[lo + c * rows : lo + (1 + c) * rows, :] = acc[here, c * D : (c + 1) * D]
        dst[lo + 3 * rows : lo + 3 * rows + BIAS, :] = lines[...]

    send_slots(copies, n, outs, 3 * rows + BIAS, put, True)


def mixed_body(first, copies, ins, outs, bufs):
    z_h, wd_h, x2_h, bias, live = ins[:5]
    z, wd, x2, mixed = bufs
    t = mixed.shape[0]
    tile = 256
    wd, x2 = Held(copies, wd_h, wd), Held(copies, x2_h.at[pl.ds(first, t), :], x2)
    zs = [
        copies.start(z_h.at[pl.ds(first + i * tile, tile), :], z.at[pl.ds(i * tile, tile), :]) for i in range(t // tile)
    ]
    cols = jnp.broadcast_to(live[:, first : first + t].astype(F32), (128, t)).T
    wd, x2 = wd.ref, x2.ref

    def product(i):
        zs[i].wait()
        return mm(z[i * tile : (i + 1) * tile, :], wd[...], NN)

    def use(i, got):
        at = slice(i * tile, (i + 1) * tile)
        out = x2[at, :] + got + bias[DBI : DBI + 1, :]
        mixed[at, :] = jnp.where(cols[at, :1] >= 0, out, 0.0).astype(BF)
        copies.send(mixed.at[pl.ds(i * tile, tile), :], outs[0].at[pl.ds(first + i * tile, tile), :])

    staggered([(i,) for i in range(t // tile)], product, use)


def on_device(n, d, tokens, segments, cotangent, w_qkv, w_out, w_up, w_down, *vectors):
    t = tokens.shape[0]
    rows = w_qkv.shape[0]
    fr = w_down.shape[0]
    nb, nh = t // DB, HALF // DB
    me = lax.axis_index("fsdp")
    qb, vb, ob, ub, db, g1, c1, g2, c2 = vectors
    lines = [qb, vb, ob, db, g1, c1, g2, c2, ub]
    ra, rb, rc = 3 * rows + BIAS, 5 * rows, fr
    pack_a, pack_b = run(
        functools.partial(pack_body, n),
        kind("A", w_qkv, w_out, w_up, *lines),
        [((ra, D), BF, "A"), ((rb, D), BF, "A")],
        [((ra, D), BF), ((rb, D), BF)] + [(a.shape, BF) for a in lines],
        name="pack",
        room=58,
    )
    a = Gather(pack_a, n)
    b = Gather(pack_b, n)
    got_a = a.pieces()
    c = Gather(after(w_down, a.have[1]), n)
    live = (segments >= 0)[:, None]
    gm = jnp.where(live, cotangent, jnp.zeros_like(cotangent))
    seg_row = segments[None, :]

    tok, tokt, wide = ((t, D), BF), ((D, t), BF), ((t, FF), BF)
    hrow, bias_s, tokf = ((HEADS, t), F32), ((BIAS, D), F32), ((t, D), F32)
    bias, wq, h1, q, k, v, kt, vt = run(
        functools.partial(qkv_body, n, rows),
        kind("A", tokens, *got_a),
        [o + ("V",) for o in (bias_s, ((D, 3 * D), BF), tok, tok, tok, tok, tokt, tokt)],
        [tok, ((n, BIAS, D), BF)],
        sems=96,
        flops=10**9,
        name="qkv",
        room=36,
    )
    ot, linv, e, ed = run(
        functools.partial(attn_body, n),
        kind("V", seg_row, after(q, b.have[1]), k, vt),
        [o + ("V",) for o in (tokt, hrow, ((HEADS, HALF, HALF), BF), ((HEADS, nb - nh, DB, DB), BF))],
        flops=10**9,
        name="attn",
    )
    got_b = b.pieces(ot)

    steps = len(step_bits(n)[0])
    counts = [1 << (steps - 1 - p) for p in range(steps)] + [1]

    def slots(r):
        return [((n // 2 * r, D), BF, "V")] + [((m * r, D), BF, "V") for m in counts]

    wo, wu, x2, h2, z, gd = run(
        functools.partial(mlp_up_body, n, rows),
        kind("A", tokens) + kind("V", ot, bias) + kind("A", *got_b),
        [o + ("V",) for o in (((D, D), BF), ((D, FF), BF), tokf, tok, wide, wide)],
        [tok],
        name="mlp_up",
    )
    got_c = c.pieces(h2)
    z_far, x2_far, *down = run(
        functools.partial(mlp_down_body, n),
        kind("V", z, x2) + kind("A", gm),
        [wide + ("A",), tokf + ("A",)] + slots(rc),
        [tok, ((n, rc, D), BF)],
        name="mlp_down",
    )
    down = Sum(n, d, down[0], down[1:])

    wd, gu, sums = run(
        functools.partial(mlp_back_body, n),
        kind("A", gm) + kind("V", gd) + kind("A", *got_c),
        [((FF, D), BF, "A"), wide + ("V",), bias_s + ("V",)],
        [tok, ((FF, D), BF)],
        name="mlp_back",
    )
    s = down.advance(gu)
    ga, got, drow, bg = run(
        norm_back_body,
        kind("V", after(gu, s), wu, x2, bias, wo, linv, ot, sums) + kind("A", gm),
        [o + ("V",) for o in (tok, tokt, hrow, bias_s)],
        [tok],
        name="norm_back",
    )
    up = run(
        functools.partial(mlp_grad_body, n, rows),
        kind("V", ot, ga, h2, gu),
        slots(rb),
        [((D, FF), BF), ((D, D), BF)],
        name="mlp_grad",
    )
    up_sent = up[0]
    up = Sum(n, d, up[0], up[1:])
    s = down.advance(up_sent)
    half, halft = ((HALF, D), BF), ((D, HALF), BF)
    gqt, gk, gv = run(
        functools.partial(attn_back_body, n),
        kind("V", seg_row, after(v, s), got, drow, e, kt, q),
        [o + ("V",) for o in (halft, half, half)],
        name="attn_back",
    )
    r = up.advance(gk)
    s = down.advance(gk, r)
    tokens_grad, g, lines_b = run(
        qkv_back_body,
        kind("V", after(v, s, r), got, drow, ed, kt, q, gqt, gk, gv, wq, ga) + kind("A", tokens) + kind("V", bias, bg),
        [tok + ("A",), ((t, 3 * D), BF, "V"), ((BIAS, D), BF, "V")],
        [tok, tokt, tok, tok, tok],
        name="qkv_back",
    )
    last = run(
        functools.partial(qkv_grad_body, n, rows),
        kind("V", h1, g, lines_b),
        slots(ra),
        [((D, 3 * D), BF)],
        sems=128,
        name="qkv_grad",
    )
    s = down.advance(last[0], send=False)
    last_sent = after(last[0], s)
    last = Sum(n, d, last_sent, last[1:], True)
    r = up.advance(last_sent)
    down.send_later(r)
    r = last.advance(r)
    def half_mixed(part, hold, *before):
        (out,) = run(
            functools.partial(mixed_body, part * (t // 2)),
            kind("A", after(z_far, hold), wd, x2_far) + kind("V", bias, seg_row) + kind("A", *before),
            [tok + ("A",)],
            [((t // 2, FF), BF), ((FF, D), BF), ((t // 2, D), F32), ((t // 2, D), BF)],
            name="mixed" + str(part),
            alias={5: 0} if before else None,
        )
        return out

    mixed = half_mixed(0, r)
    s = up.advance(mixed)
    r = last.advance(s)
    mixed = half_mixed(1, r, mixed)
    s = down.advance(mixed)
    r = last.advance(s)
    s = up.advance(r)
    r = last.advance(s)
    s = up.advance(r)
    r = last.advance(s)
    down, up, last = down.end(), up.end(), last.end()
    part = D // n
    first = me * part
    vec = lax.dynamic_slice(last, (3 * rows, first), (BIAS, part)).astype(F32)
    ubs = last[3 * rows + UB : 3 * rows + UB + 4]
    ubg = sum(jnp.where(me == j, ubs[j * fr // D, j * fr % D : j * fr % D + fr], 0.0) for j in range(n))
    qkv_grad = jnp.concatenate([last[c * rows : (c + 1) * rows] for c in range(3)], 1).astype(F32)
    up_grad = jnp.concatenate([up[(1 + c) * rows : (2 + c) * rows] for c in range(4)], 1).astype(F32)
    return (
        mixed,
        tokens_grad,
        qkv_grad,
        up[:rows].astype(F32),
        up_grad,
        down.astype(F32),
        vec[QB],
        vec[VB],
        vec[OB],
        ubg,
        vec[DBI],
        vec[G1],
        vec[C1],
        vec[G2],
        vec[C2],
    )


def solution(mesh):
    rows = P(("dp", "fsdp"), None)
    mat, vec = P("fsdp", None), P("fsdp")
    return jax.shard_map(
        functools.partial(on_device, mesh.shape["fsdp"], mesh.shape["dp"]),
        mesh=mesh,
        in_specs=(rows, P(("dp", "fsdp")), rows) + (mat,) * 4 + (vec,) * 9,
        out_specs=(rows, rows) + (mat,) * 4 + (vec,) * 9,
        check_vma=False,
    )
```
